32 devices in a mesh: kv: 4 (over y, x), wide: 8 (over z, core).
Axes of the slice: x: 2, y: 2, z: 4, core: 2. Of those that a mesh axis runs over, the one named last changes fastest.
Arguments:
- stream_in: bfloat16 [16, 4, 2560], P('wide', None, 'kv'), may hold values from -8 to 8
- queries: bfloat16 [16, 4, 2560], P('wide', None, 'kv'), may hold values from -2.5 to 2.5
- new_kv: bfloat16 [16, 4, 2, 512], P('wide', None, None, 'kv'), may hold values from -2.5 to 2.5
- cache_keys: bfloat16 [4, 128, 128, 128], P('kv', 'wide'), may hold values from -2.5 to 2.5
- cache_values: bfloat16 [4, 128, 128, 128], P('kv', 'wide'), may hold values from -2.5 to 2.5
- lengths: int32 [2], replicated, may hold values from 1 to 4096, as said below
- page_table: int32 [2, 32], replicated, may hold values from -1 to 127, as said below
- parents: int32 [16, 3], replicated, may hold values from 0 to 7
- routes: int32 [16, 4, 6], P('wide'), may hold values from 0 to 63, all different within a row; in each aligned block of 8 rows (0 to 7, 8 to 15, ..., all dimensions but the last counted through in order) at most 2 rows name the same one
- norm_gain: float32 [2560], replicated, may hold values from 0.5 to 1.5
- router: bfloat16 [2560, 64], replicated, may hold values from -0.01965332 to 0.01965332
- gate_w: bfloat16 [128, 2560, 768], P('wide', None, 'kv'), may hold values from -0.125 to 0.125
- up_w: bfloat16 [128, 2560, 768], P('wide', None, 'kv'), may hold values from -0.125 to 0.125
- down_w: bfloat16 [128, 768, 2560], P('wide', 'kv'), may hold values from -0.15625 to 0.15625
Outputs:
- stream_out: bfloat16 [16, 4, 2560], P('wide', None, 'kv')
The draws below stay inside these ranges and needn't reach their ends.
Inputs may be any that keep to these rules, and one draw needn't show every extreme that they name: `lengths`: one group has exactly 4096 positions. `page_table`: entry [g, b] is the slot (index of wide times 16 plus the local slot) holding positions b * 128 to b * 128 + 127 of group g when b * 128 < lengths[g], and -1 otherwise; no slot is named twice; every slot of some index of wide is named. `parents`: entry [t, j] is a beam of t's own group. `routes`: within the rows of one index of wide (2 beams times 4 steps) no expert is named by more than 2 rows.
All inputs are finite; a program needn't handle non-finite values.
Results may differ from the reference program's by a relative error of at most 0.012.
Values may be sent and summed in bfloat16 or wider, within the bound.
No kernel may reach another device: no remote copies, remote signals or barrier semaphores. Data moves between devices by JAX's collectives and lax.ppermute only.
A program may use at most 128 MiB of HBM per device.

```python
import math
import jax
import jax.numpy as jnp
import numpy as np
from jax import lax

D = 2560
QH = 20
KVH = 4
HD = 128
E = 64
FF = 1536
TOP = 6
BEAMS = 8
STEPS = 4
STEP_TOK = 2
BLK = 128
MAXLEN = 4096
MAXB = 32
SLOTS_DEV = 16
SLOTS_ALL = 128
GROUPS = 2
TOKENS = 16
MOST = 2
N_WIDE = 8


def cache_layout(key):
    subkeys = jax.random.split(jax.random.fold_in(key, 41), 5)
    exponents = jax.random.randint(subkeys[0], (GROUPS,), 0, 14)
    span_cap = jnp.minimum(jnp.left_shift(jnp.ones((GROUPS,), jnp.int32), exponents), MAXLEN)
    raw_draw = jax.random.randint(subkeys[1], (GROUPS,), 0, MAXLEN)
    group_sizes = 1 + raw_draw % span_cap
    longest = jax.random.randint(subkeys[2], (), 0, GROUPS)
    group_sizes = jnp.where(jnp.arange(GROUPS) == longest, MAXLEN, group_sizes)
    block_used = jnp.arange(MAXB)[None, :] * BLK < group_sizes[:, None]
    flat_used = block_used.reshape(-1)
    used_rank = jnp.cumsum(flat_used.astype(jnp.int32)) - 1
    shuffle = jax.random.permutation(subkeys[3], SLOTS_ALL)
    full_device = jax.random.randint(subkeys[4], (), 0, SLOTS_ALL // SLOTS_DEV)
    slot_ids = jnp.arange(SLOTS_ALL)
    slot_score = shuffle + jnp.where(slot_ids // SLOTS_DEV == full_device, 0, SLOTS_ALL)
    slot_order = jnp.argsort(slot_score, stable=True)
    page_rows = jnp.where(flat_used, slot_order[jnp.maximum(used_rank, 0)], -1)
    return (group_sizes.astype(jnp.int32), page_rows.reshape(GROUPS, MAXB).astype(jnp.int32))


def draw_lengths(key, part):
    return cache_layout(key)[0]


def draw_page_table(key, part):
    return cache_layout(key)[1]


def draw_stream_in(key, part):
    subkeys = jax.random.split(jax.random.fold_in(key, 5), 1)
    normal_base = jax.random.normal(subkeys[0], (TOKENS, STEPS, D), jnp.float32)
    return jnp.clip(normal_base, -8.0, 8.0).astype(jnp.bfloat16)


def place_ends(result, own_key, smallest, largest):
    longest = result.shape.index(max(result.shape))
    spots = []
    for shift in (0, 1):
        where = [jax.random.randint(jax.random.fold_in(own_key, axis), (), 0, length) for axis, length in enumerate(result.shape)]
        where[longest] = (where[longest] + shift) % result.shape[longest]
        spots.append(tuple(where))
    return result.at[spots[0]].set(smallest).at[spots[1]].set(largest)


def shard_levels(own_key, extent, pieces, smallest, largest):
    def one(axis_at, parts):
        draws = jax.random.uniform(jax.random.fold_in(jax.random.fold_in(own_key, 6), axis_at), (parts,), jnp.float32, smallest / len(pieces), largest / len(pieces))
        return jnp.repeat(jnp.exp(draws), extent[axis_at] // parts).reshape((-1,) + (1,) * (len(extent) - axis_at - 1))

    loudness = one(*pieces[0])
    for cut in pieces[1:]:
        loudness = loudness * one(*cut)
    return loudness


def routed_block(own_key, own, number, rows, amount, top, most, slope):
    sequence = jax.random.permutation(own_key, amount)
    heavy_load, usual = shares(amount, rows * top, most, slope, True), shares(amount, rows * top, most, slope, False)
    places = jnp.arange(amount)

    def named(sizes, offset_by):
        used = int((sizes > 0).sum())
        fixed = max(1, used // 4)
        shifted = fixed + (places - fixed + offset_by * (used - fixed)) % max(1, amount - fixed)
        return jnp.zeros((amount,), jnp.int32).at[sequence[jnp.where(places < fixed, places, shifted)]].set(jnp.asarray(sizes, jnp.int32))

    sizes = jnp.where(number % 4 == 0, named(heavy_load, number // 4), named(usual, number - number // 4 - 1))
    mixed = jax.random.permutation(jax.random.fold_in(own, 3), amount)
    donor, sink = mixed[0:amount // 2 * 2:2], mixed[1:amount // 2 * 2:2]
    slack = jnp.minimum(sizes[donor] - 1, most - sizes[sink]) // 2
    slack = jnp.where((donor == sequence[0]) | (sink == sequence[0]) | (sizes[sink] == 0), 0, jnp.maximum(slack, 0))
    shifted = jax.random.randint(jax.random.fold_in(own, 4), (amount // 2,), 0, 1 << 20) % (slack + 1)
    sizes = sizes.at[donor].add(-shifted).at[sink].add(shifted)
    members = jnp.searchsorted(jnp.cumsum(sizes), jnp.arange(rows * top), side="right").astype(jnp.int32)
    grid = members.reshape(top, rows).T
    grid = grid[jax.random.permutation(jax.random.fold_in(own, 1), rows)]
    offset_by = jax.random.randint(jax.random.fold_in(own, 2), (rows, 1), 0, top)
    return jnp.take_along_axis(grid, (jnp.arange(top)[None, :] + offset_by) % top, axis=1)


def shares(amount, total, reach, skew, full):
    weights = [(1 << 20) // math.isqrt(grade ** skew) + 1 for grade in range(1, amount + 1)]
    largest = reach if full else min(reach, max(-(-total // amount), total * weights[0] // sum(weights)))
    least = 1 if total - largest >= amount - 1 else 0
    counts, rest = [largest] + [least] * (amount - 1), total - largest - least * (amount - 1)
    while rest > 0:
        free = [i for i in range(1, amount) if counts[i] < largest] or [i for i in range(1, amount) if counts[i] < reach]
        whole, left = sum([weights[i] for i in free]), rest
        for i in free:
            addition = min(reach - counts[i], max(1, left * weights[i] // whole), rest)
            counts[i] = counts[i] + addition
            rest = rest - addition
    return np.array(counts)


def centred(rng, extent, spread, limit, cuts=(), kind=jnp.bfloat16):
    drawn = spread * jax.random.normal(rng, extent, jnp.float32)
    if cuts:
        drawn = drawn * shard_levels(rng, extent, cuts, -0.22, 0.18)
    return jnp.clip(drawn, -limit, limit).astype(kind)


def setup_inputs(seed: int = 0) -> dict:
    seeds = jax.random.split(jax.random.key(seed), 15)
    stream_in = draw_stream_in(jax.random.fold_in(seeds[14], 71), 0)
    queries = centred(seeds[1], (TOKENS, STEPS, QH * HD), 1.0, 2.5, ((0, 8), (2, 4)))
    new_kv = centred(seeds[2], (TOKENS, STEPS, 2, KVH * HD), 1.0, 2.5, ((0, 8), (3, 4)))
    cache_keys = centred(seeds[3], (KVH, SLOTS_ALL, BLK, HD), 1.0, 2.5, ((0, 4), (1, 8)))
    cache_values = centred(seeds[4], (KVH, SLOTS_ALL, BLK, HD), 1.0, 2.5, ((0, 4), (1, 8)))
    lengths = draw_lengths(jax.random.fold_in(seeds[14], 71), 0)
    page_table = draw_page_table(jax.random.fold_in(seeds[14], 71), 0)
    parents = place_ends(jax.random.randint(seeds[7], (TOKENS, STEPS - 1), 0, BEAMS), jax.random.fold_in(seeds[7], 1), 0, BEAMS - 1).astype(jnp.int32)
    routes_keys = jax.random.split(jax.random.fold_in(seeds[8], 1), TOKENS * STEPS // (STEPS * STEP_TOK))
    routes_turns = jax.random.permutation(jax.random.fold_in(seeds[8], 3), TOKENS * STEPS // (STEPS * STEP_TOK))
    routes = jax.vmap(lambda own, number: routed_block(jax.random.fold_in(seeds[8], 2), own, number, STEPS * STEP_TOK, E, TOP, MOST, 2))(routes_keys, routes_turns).reshape((TOKENS, STEPS, TOP))
    norm_gain = jnp.clip(1.0 + 0.1 * jax.random.normal(seeds[9], (D,), jnp.float32), 0.5, 1.5)
    router = jnp.clip(jax.random.uniform(seeds[10], (D, E), jnp.float32, -0.01965332, 0.01965332), -0.01965332, 0.01965332).astype(jnp.bfloat16)
    gate_w = centred(seeds[11], (2 * E, D, FF // 2), D ** -0.5, 0.125, ((0, 8), (2, 4)))
    up_w = centred(seeds[12], (2 * E, D, FF // 2), D ** -0.5, 0.125, ((0, 8), (2, 4)))
    down_w = centred(seeds[13], (2 * E, FF // 2, D), FF ** -0.5, 0.15625, ((0, 8), (1, 4)))
    return dict(stream_in=stream_in, queries=queries, new_kv=new_kv, cache_keys=cache_keys, cache_values=cache_values, lengths=lengths, page_table=page_table, parents=parents, routes=routes, norm_gain=norm_gain, router=router, gate_w=gate_w, up_w=up_w, down_w=down_w)


def chain_tokens(parents):
    tokens = jnp.arange(TOKENS, dtype=jnp.int32)
    group_base = tokens // BEAMS * BEAMS
    chain_table = []
    for step_now in range(STEPS):
        columns = [tokens] * STEPS
        current = tokens
        for earlier in range(step_now, 0, -1):
            current = (group_base + parents[current, earlier - 1]).astype(jnp.int32)
            columns[earlier - 1] = current
        chain_table.append(jnp.stack(columns, axis=1))
    return jnp.stack(chain_table, axis=1)

def reference(stream_in, queries, new_kv, cache_keys, cache_values, lengths, page_table, parents, routes, norm_gain, router, gate_w, up_w, down_w):
    score_scale = 1.0 / math.sqrt(HD)
    head_ratio = QH // KVH
    chains = chain_tokens(parents)
    history = new_kv[chains, jnp.arange(STEPS, dtype=jnp.int32)[None, None, :]]
    causal = (jnp.arange(STEPS)[None, :] <= jnp.arange(STEPS)[:, None]).astype(jnp.float32)
    positions = jnp.arange(MAXLEN, dtype=jnp.int32)

    def one_group(group_id):
        first_token = (group_id * BEAMS).astype(jnp.int32)
        group_queries = lax.dynamic_slice_in_dim(queries, first_token, BEAMS, 0).astype(jnp.float32)
        group_queries = group_queries.reshape(BEAMS, STEPS, KVH, head_ratio, HD)
        page_rows = jnp.maximum(page_table[group_id], 0)
        block_keys = cache_keys[:, page_rows].reshape(KVH, MAXLEN, HD).astype(jnp.float32)
        block_values = cache_values[:, page_rows].reshape(KVH, MAXLEN, HD).astype(jnp.float32)
        valid_mask = (positions < lengths[group_id]).astype(jnp.float32)
        scores = jnp.einsum('bskrd,kpd->bskrp', group_queries, block_keys)
        weights = (jnp.exp(scores * score_scale) * valid_mask).astype(jnp.bfloat16)
        weights = lax.optimization_barrier(weights).astype(jnp.float32)
        numerator = jnp.einsum('bskrp,kpd->bskrd', weights, block_values)
        denominator = lax.optimization_barrier(jnp.sum(weights, axis=-1))
        past_rows = lax.dynamic_slice_in_dim(history, first_token, BEAMS, 0).astype(jnp.float32)
        tail_keys = past_rows[:, :, :, 0].reshape(BEAMS, STEPS, STEPS, KVH, HD)
        tail_values = past_rows[:, :, :, 1].reshape(BEAMS, STEPS, STEPS, KVH, HD)
        tail_scores = jnp.einsum('bskrd,bsjkd->bskrj', group_queries, tail_keys)
        tail_weights = (jnp.exp(tail_scores * score_scale) * causal[None, :, None, None, :]).astype(jnp.bfloat16)
        tail_weights = lax.optimization_barrier(tail_weights).astype(jnp.float32)
        numerator = numerator + jnp.einsum('bskrj,bsjkd->bskrd', tail_weights, tail_values)
        denominator = denominator + lax.optimization_barrier(jnp.sum(tail_weights, axis=-1))
        attended = (numerator / denominator[..., None]).astype(jnp.bfloat16)
        return attended.reshape(BEAMS, STEPS, QH * HD)
    attended = lax.map(one_group, jnp.arange(GROUPS, dtype=jnp.int32)).reshape(TOKENS, STEPS, D)
    residual = (stream_in.astype(jnp.float32) + attended.astype(jnp.float32)).astype(jnp.bfloat16)
    row_count = TOKENS * STEPS
    token_rows = residual.reshape(row_count, D).astype(jnp.float32)
    mean_square = lax.optimization_barrier(jnp.mean(token_rows * token_rows, axis=1, keepdims=True))
    normed = (token_rows * lax.rsqrt(mean_square + 1e-06) * norm_gain[None, :]).astype(jnp.bfloat16)
    logits = jnp.dot(normed, router, preferred_element_type=jnp.float32)
    routed = routes.reshape(row_count, TOP)
    chosen = jnp.take_along_axis(logits, routed, axis=1)
    raised = jnp.exp(chosen)
    gate_share = raised / lax.optimization_barrier(jnp.sum(raised, axis=1, keepdims=True))
    capacity = N_WIDE * MOST
    padded = jnp.concatenate([normed, jnp.zeros((1, D), jnp.bfloat16)], axis=0)

    def add_expert(summed, expert):
        expert_hit = routed == expert
        weight = lax.optimization_barrier(jnp.sum(jnp.where(expert_hit, gate_share, 0.0), axis=1))
        expert_used = jnp.any(expert_hit, axis=1)
        row_index = jnp.nonzero(expert_used, size=capacity, fill_value=row_count)[0].astype(jnp.int32)
        expert_rows = padded[row_index]
        gate_full = jnp.concatenate([gate_w[2 * expert], gate_w[2 * expert + 1]], axis=1)
        up_full = jnp.concatenate([up_w[2 * expert], up_w[2 * expert + 1]], axis=1)
        down_full = jnp.concatenate([down_w[2 * expert], down_w[2 * expert + 1]], axis=0)
        gate_out = jnp.dot(expert_rows, gate_full, preferred_element_type=jnp.float32)
        up_out = jnp.dot(expert_rows, up_full, preferred_element_type=jnp.float32)
        hidden = (jax.nn.silu(gate_out) * up_out).astype(jnp.bfloat16)
        expert_out = jnp.dot(hidden, down_full, preferred_element_type=jnp.float32)
        weight_pad = jnp.concatenate([weight, jnp.zeros((1,), jnp.float32)])
        return (summed.at[row_index].add(expert_out * weight_pad[row_index][:, None]), None)
    summed, unused = lax.scan(add_expert, jnp.zeros((row_count + 1, D), jnp.float32), jnp.arange(E, dtype=jnp.int32))
    mixed_rows = (residual.reshape(row_count, D).astype(jnp.float32) + summed[:row_count]).astype(jnp.bfloat16)
    return mixed_rows.reshape(TOKENS, STEPS, D)
```

```python
import math

import jax
import jax.numpy as jnp
from jax import lax
from jax.sharding import PartitionSpec as P

HD = 128
E = 64
BEAMS = 8
BLK = 128
LANES = 128


def spread(block, axes, count):
    copies = jnp.broadcast_to(block[None], (count,) + block.shape)
    return lax.all_to_all(copies, axes, split_axis=0, concat_axis=0, tiled=True)


def chain_mask(parents, own_tokens, steps):
    tokens = jnp.arange(parents.shape[0], dtype=jnp.int32)
    base = tokens // BEAMS * BEAMS
    hops = [
        ((base + parents[:, j])[:, None] == tokens[None, :]).astype(jnp.float32)
        for j in range(steps - 1)
    ]
    same = (own_tokens[:, None] == tokens[None, :]).astype(jnp.float32)
    zero = jnp.zeros_like(same)
    rows = []
    for step_now in range(steps):
        cells = [zero] * steps
        cells[step_now] = same
        for earlier in range(step_now, 0, -1):
            cells[earlier - 1] = jnp.dot(cells[earlier], hops[earlier - 1])
        rows.append(jnp.stack(cells, axis=1))
    return jnp.stack(rows, axis=1)


def local(
    stream_in,
    queries,
    new_kv,
    cache_keys,
    cache_values,
    lengths,
    page_table,
    parents,
    routes,
    norm_gain,
    router,
    gate_w,
    up_w,
    down_w,
):
    wide_index = lax.axis_index("wide")
    wide_count = lax.axis_size("wide")
    kv_count = lax.axis_size("kv")
    step_tok, steps, feats = stream_in.shape
    rows = step_tok * steps
    heads = feats // HD
    groups = lengths.shape[0]
    token_count = groups * BEAMS
    all_rows = token_count * steps
    slots_local = cache_keys.shape[1]
    top = routes.shape[2]
    halves = gate_w.shape[0]
    score_scale = 1.0 / math.sqrt(HD)

    packed = jnp.concatenate(
        [
            queries.reshape(rows, feats),
            new_kv.reshape(rows, 2 * HD),
            jnp.pad(routes.reshape(rows, top).astype(jnp.bfloat16), ((0, 0), (0, LANES - top))),
        ],
        axis=1,
    )
    gathered = spread(packed, "wide", wide_count).reshape(all_rows, feats + 2 * HD + LANES)
    all_queries = gathered[:, :feats]
    all_keys = gathered[:, feats : feats + HD]
    all_values = gathered[:, feats + HD : feats + 2 * HD]
    all_routes = gathered[:, feats + 2 * HD : feats + 2 * HD + top].astype(jnp.int32)

    slot_ids = wide_index * slots_local + jnp.arange(slots_local, dtype=jnp.int32)
    slot_hits = page_table[None, :, :] == slot_ids[:, None, None]
    group_ids = jnp.arange(groups, dtype=jnp.int32)
    block_starts = jnp.arange(page_table.shape[1], dtype=jnp.int32) * BLK
    owner_group = jnp.sum(jnp.where(slot_hits, group_ids[None, :, None], 0), axis=(1, 2))
    block_limit = jnp.sum(
        jnp.where(slot_hits, lengths[None, :, None] - block_starts[None, None, :], 0), axis=(1, 2)
    )
    key_ok = (jnp.arange(BLK, dtype=jnp.int32)[None, :] < block_limit[:, None]).astype(jnp.float32)
    grouped = all_queries.reshape(groups, BEAMS * steps * heads, HD)
    picked = grouped[owner_group]
    scores = jnp.einsum("nrd,npd->nrp", picked, cache_keys[0], preferred_element_type=jnp.float32)
    weights = (jnp.exp(scores * score_scale) * key_ok[:, None, :]).astype(jnp.bfloat16)
    numerator = jnp.einsum(
        "nrp,npd->nrd", weights, cache_values[0], preferred_element_type=jnp.float32
    )
    denominator = jnp.sum(weights.astype(jnp.float32), axis=-1)
    member = (owner_group[None, :] == group_ids[:, None]).astype(jnp.float32)
    part_num = jnp.sum(member[:, :, None, None] * numerator[None], axis=1)
    part_den = jnp.sum(member[:, :, None] * denominator[None], axis=1)
    part_den = part_den.reshape(all_rows, heads)
    den_high = part_den.astype(jnp.bfloat16)
    den_low = (part_den - den_high.astype(jnp.float32)).astype(jnp.bfloat16)
    sums = jnp.concatenate(
        [
            part_num.reshape(all_rows, feats).astype(jnp.bfloat16),
            jnp.pad(
                jnp.concatenate([den_high, den_low], axis=1), ((0, 0), (0, LANES - 2 * heads))
            ),
        ],
        axis=1,
    )
    arrived = lax.all_to_all(
        sums.reshape(wide_count, rows, feats + LANES), "wide", split_axis=0, concat_axis=0, tiled=True
    )
    total = jnp.sum(arrived.astype(jnp.float32), axis=0)
    mine_num = total[:, :feats].reshape(rows, heads, HD)
    mine_den = total[:, feats : feats + heads] + total[:, feats + heads : feats + 2 * heads]

    own_tokens = wide_index * step_tok + jnp.arange(step_tok, dtype=jnp.int32)
    mask = chain_mask(parents, own_tokens, steps).reshape(rows, 1, steps, token_count)
    own_queries = queries.reshape(rows, heads, HD)
    tail_keys = all_keys.reshape(token_count, steps, HD)
    tail_values = all_values.reshape(token_count, steps, HD)
    tail_scores = jnp.einsum(
        "rhd,tjd->rhjt", own_queries, tail_keys, preferred_element_type=jnp.float32
    )
    tail_weights = jnp.where(mask > 0, jnp.exp(tail_scores * score_scale), 0.0)
    tail_weights = tail_weights.astype(jnp.bfloat16)
    tail_num = jnp.einsum(
        "rhjt,tjd->rhd", tail_weights, tail_values, preferred_element_type=jnp.float32
    )
    tail_den = jnp.sum(tail_weights.astype(jnp.float32), axis=(2, 3))
    attended = ((mine_num + tail_num) / (mine_den + tail_den)[..., None]).astype(jnp.bfloat16)
    residual = (
        stream_in.reshape(rows, feats).astype(jnp.float32)
        + attended.reshape(rows, feats).astype(jnp.float32)
    ).astype(jnp.bfloat16)

    spread_rows = spread(residual, ("kv", "wide"), kv_count * wide_count)
    spread_rows = spread_rows.reshape(kv_count, all_rows, feats)
    token_rows = jnp.swapaxes(spread_rows, 0, 1).reshape(all_rows, kv_count * feats)
    token_rows = token_rows.astype(jnp.float32)
    mean_square = jnp.mean(token_rows * token_rows, axis=1, keepdims=True)
    normed = (token_rows * lax.rsqrt(mean_square + 1e-06) * norm_gain[None, :]).astype(jnp.bfloat16)
    logits = jnp.dot(normed, router, preferred_element_type=jnp.float32)
    expert_ids = jnp.arange(E, dtype=jnp.int32)
    chosen = jnp.any(all_routes[:, :, None] == expert_ids[None, None, :], axis=1)
    raised = jnp.where(chosen, jnp.exp(logits), 0.0)
    share = raised / jnp.sum(raised, axis=1, keepdims=True)
    half_expert = (wide_index * halves + jnp.arange(halves, dtype=jnp.int32)) // 2
    pick = (expert_ids[:, None] == half_expert[None, :]).astype(jnp.float32)
    half_share = jnp.dot(share, pick, precision=lax.Precision.HIGHEST)

    gate_out = jnp.einsum("td,ldf->tlf", normed, gate_w, preferred_element_type=jnp.float32)
    up_out = jnp.einsum("td,ldf->tlf", normed, up_w, preferred_element_type=jnp.float32)
    hidden = (jax.nn.silu(gate_out) * up_out * half_share[:, :, None]).astype(jnp.bfloat16)
    partial = jnp.einsum("tlf,lfd->td", hidden, down_w, preferred_element_type=jnp.float32)
    outgoing = partial.astype(jnp.bfloat16).reshape(wide_count, rows, kv_count, feats)
    outgoing = jnp.transpose(outgoing, (2, 0, 1, 3)).reshape(kv_count * wide_count, rows, feats)
    returned = lax.all_to_all(
        outgoing, ("kv", "wide"), split_axis=0, concat_axis=0, tiled=True
    )
    moe_part = jnp.sum(returned.astype(jnp.float32), axis=0)
    out = (residual.astype(jnp.float32) + moe_part).astype(jnp.bfloat16)
    return out.reshape(step_tok, steps, feats)


def solution(mesh):
    return jax.shard_map(
        local,
        mesh=mesh,
        in_specs=(
            P("wide", None, "kv"),
            P("wide", None, "kv"),
            P("wide", None, None, "kv"),
            P("kv", "wide", None, None),
            P("kv", "wide", None, None),
            P(),
            P(),
            P(),
            P("wide", None, None),
            P(),
            P(),
            P("wide", None, "kv"),
            P("wide", None, "kv"),
            P("wide", "kv", None),
        ),
        out_specs=P("wide", None, "kv"),
        check_vma=False,
    )
```

```python
import functools
import math

import jax
import jax.numpy as jnp
from jax import lax
from jax.experimental import pallas as pl
from jax.experimental.pallas import tpu as pltpu
from jax.sharding import PartitionSpec as P

HD = 128
E = 64
BEAMS = 8
BLK = 128
LANES = 128
MIB = 2**20
AHEAD = 6
F32 = jnp.float32
BF16 = jnp.bfloat16
NT = (((1,), (1,)), ((), ()))
TN = (((0,), (0,)), ((), ()))
VMEM = pl.BlockSpec(memory_space=pltpu.VMEM)
SMEM = pl.BlockSpec(memory_space=pltpu.SMEM)
HBM = pl.BlockSpec(memory_space=pltpu.HBM)


def sent(block, axes):
    return lax.all_to_all(block, axes, split_axis=0, concat_axis=0, tiled=True)


def pack_kernel(query_ref, new_ref, route_ref, out_ref):
    step_tok, steps, feats = query_ref.shape
    lanes = lax.broadcasted_iota(jnp.int32, (steps, LANES), 1)
    parts = []
    for t in range(step_tok):
        named = route_ref[t]
        chosen = jnp.zeros((steps, LANES), F32)
        for i in range(named.shape[1]):
            chosen = jnp.where(named[:, i : i + 1] == lanes, 1.0, chosen)
        parts.append(
            jnp.concatenate(
                [
                    query_ref[t].astype(F32),
                    new_ref[t, :, 0, :].astype(F32),
                    new_ref[t, :, 1, :].astype(F32),
                    chosen,
                ],
                axis=1,
            )
        )
    block = jnp.concatenate(parts, axis=0).astype(BF16)
    for w in range(out_ref.shape[0]):
        out_ref[w] = block


def attend_kernel(owner_ref, limit_ref, rows_ref, key_ref, value_ref, out_ref, query_ref, sum_ref):
    slots = key_ref.shape[0]
    groups, stacked, _ = query_ref.shape
    feats = out_ref.shape[1] - LANES
    heads = feats // HD
    span = stacked // heads
    scale = 1.0 / math.sqrt(HD)
    for g in range(groups):
        for h in range(heads):
            query_ref[g, h * span : (h + 1) * span, :] = rows_ref[
                g * span : (g + 1) * span, h * HD : (h + 1) * HD
            ]
    sum_ref[...] = jnp.zeros_like(sum_ref)
    ones = jnp.ones((BLK, HD), BF16)
    place = lax.broadcasted_iota(jnp.int32, (stacked, BLK), 1)
    for n in range(slots):
        group = owner_ref[n]
        scores = lax.dot_general(query_ref[group], key_ref[n], NT, preferred_element_type=F32)
        weights = jnp.where(place < limit_ref[n], jnp.exp(scores * scale), 0.0).astype(BF16)
        extended = jnp.concatenate([value_ref[n], ones], axis=1)
        sum_ref[group] += jnp.dot(weights, extended, preferred_element_type=F32)
    lanes = lax.broadcasted_iota(jnp.int32, (span, LANES), 1)
    for g in range(groups):
        tail = jnp.zeros((span, LANES), F32)
        for h in range(heads):
            piece = sum_ref[g, h * span : (h + 1) * span, :]
            out_ref[g * span : (g + 1) * span, h * HD : (h + 1) * HD] = piece[:, :HD].astype(BF16)
            high = piece[:, HD:].astype(BF16).astype(F32)
            tail = jnp.where(lanes == h, high, tail)
            tail = jnp.where(lanes == heads + h, piece[:, HD:] - high, tail)
        out_ref[g * span : (g + 1) * span, feats:] = tail.astype(BF16)


def suffix_kernel(query_ref, rows_ref, mask_ref, num_ref, den_ref):
    step_tok, steps, feats = query_ref.shape
    rows = step_tok * steps
    heads = feats // HD
    scale = 1.0 / math.sqrt(HD)
    own = jnp.concatenate([query_ref[t].astype(F32) for t in range(step_tok)], axis=0)
    stacked = jnp.concatenate([own[:, h * HD : (h + 1) * HD] for h in range(heads)], axis=0)
    keys = rows_ref[:, feats : feats + HD]
    values = rows_ref[:, feats + HD : feats + 2 * HD]
    scores = lax.dot_general(stacked.astype(BF16), keys, NT, preferred_element_type=F32)
    mask = jnp.concatenate([mask_ref[...]] * heads, axis=0)
    weights = jnp.where(mask > 0, jnp.exp(scores * scale), 0.0).astype(BF16)
    extended = jnp.concatenate([values, jnp.ones_like(values)], axis=1)
    sums = jnp.dot(weights, extended, preferred_element_type=F32)
    for h in range(heads):
        num_ref[:, h * HD : (h + 1) * HD] = sums[h * rows : (h + 1) * rows, :HD]
        den_ref[:, h * HD : (h + 1) * HD] = sums[h * rows : (h + 1) * rows, HD:]


def residual_kernel(sums_ref, num_ref, den_ref, stream_ref, out_ref, spread_ref):
    rows, feats = out_ref.shape
    heads = feats // HD
    total = sums_ref[0].astype(F32)
    for w in range(1, sums_ref.shape[0]):
        total = total + sums_ref[w].astype(F32)
    stream = jnp.concatenate(
        [stream_ref[t].astype(F32) for t in range(stream_ref.shape[0])], axis=0
    )
    dens = total[:, feats : feats + heads] + total[:, feats + heads : feats + 2 * heads]
    parts = []
    for h in range(heads):
        at = slice(h * HD, (h + 1) * HD)
        attended = (total[:, at] + num_ref[:, at]) / (dens[:, h : h + 1] + den_ref[:, at])
        parts.append(stream[:, at] + attended.astype(BF16).astype(F32))
    residual = jnp.concatenate(parts, axis=1).astype(BF16)
    out_ref[...] = residual
    for d in range(spread_ref.shape[0]):
        spread_ref[d] = residual


def expert_kernel(
    per_unit, first_ref, rows_ref, chosen_ref, gain_ref, router_ref, gate_hbm, up_hbm, down_hbm,
    out_ref, slot_ref, norm_ref, share_ref, hidden_ref, total_ref, sems,
):
    kv_count, count, feats = rows_ref.shape
    units, width, _ = gate_hbm.shape
    sources = [ref.at[l] for l in range(units) for ref in (gate_hbm, up_hbm)]
    sources += [down_hbm.at[l] for l in range(units)]
    copies = [
        pltpu.make_async_copy(source, slot_ref.at[i], sems.at[i])
        for i, source in enumerate(sources)
    ]
    for copy in copies[:AHEAD]:
        copy.start()

    def arrive(i):
        copies[i].wait()
        if i + AHEAD < len(copies):
            copies[i + AHEAD].start()

    block = 64
    offset = chosen_ref.shape[1] - LANES
    for b in range(count // block):
        at = slice(b * block, (b + 1) * block)
        squares = jnp.zeros((block, 1), F32)
        for k in range(kv_count):
            part = rows_ref[k, at, :].astype(F32)
            squares += jnp.sum(part * part, axis=1, keepdims=True)
        root = lax.rsqrt(squares / (kv_count * feats) + 1e-06)
        for k in range(kv_count):
            columns = slice(k * feats, (k + 1) * feats)
            part = rows_ref[k, at, :].astype(F32)
            norm_ref[at, columns] = (part * root * gain_ref[:, columns]).astype(BF16)
        logits = lax.dot_general(norm_ref[at, :], router_ref[...], NT, preferred_element_type=F32)
        chosen = chosen_ref[at, offset:].astype(F32)
        raised = jnp.where(chosen[:, :E] > 0, jnp.exp(logits), 0.0)
        share = raised / jnp.sum(raised, axis=1, keepdims=True)
        share = jnp.concatenate([share, jnp.zeros((block, LANES - E), F32)], axis=1)
        share_ref[:, at] = share.T
    normed = norm_ref[...]
    for l in range(units):
        arrive(2 * l)
        arrive(2 * l + 1)
        gate = lax.dot_general(slot_ref[2 * l], normed, NT, preferred_element_type=F32)
        up = lax.dot_general(slot_ref[2 * l + 1], normed, NT, preferred_element_type=F32)
        weight = share_ref[pl.ds((first_ref[0] + l * per_unit) // 2, 1), :]
        hidden_ref[l] = (gate / (1.0 + jnp.exp(-gate)) * up * weight).astype(BF16)
    for l in range(units):
        i = 2 * units + l
        arrive(i)
        for k in range(kv_count):
            columns = slice(k * feats, (k + 1) * feats)
            piece = lax.dot_general(
                hidden_ref[l], slot_ref[i, :, columns], TN, preferred_element_type=F32
            )
            if l > 0:
                piece = piece + total_ref[k]
            if l + 1 < units:
                total_ref[k] = piece
            else:
                out_ref[k] = piece.astype(BF16)


def chain_mask(parents, own_tokens, steps):
    tokens = jnp.arange(parents.shape[0], dtype=jnp.int32)
    base = tokens // BEAMS * BEAMS
    hops = [
        ((base + parents[:, j])[:, None] == tokens[None, :]).astype(jnp.float32)
        for j in range(steps - 1)
    ]
    same = (own_tokens[:, None] == tokens[None, :]).astype(jnp.float32)
    zero = jnp.zeros_like(same)
    rows = []
    for step_now in range(steps):
        cells = [zero] * steps
        cells[step_now] = same
        for earlier in range(step_now, 0, -1):
            cells[earlier - 1] = jnp.dot(cells[earlier], hops[earlier - 1])
        rows.append(jnp.stack(cells, axis=1))
    return jnp.stack(rows, axis=1)


def local(
    stream_in,
    queries,
    new_kv,
    cache_keys,
    cache_values,
    lengths,
    page_table,
    parents,
    routes,
    norm_gain,
    router,
    gate_w,
    up_w,
    down_w,
):
    wide_index = lax.axis_index("wide")
    wide_count = lax.axis_size("wide")
    kv_count = lax.axis_size("kv")
    step_tok, steps, feats = stream_in.shape
    rows = step_tok * steps
    heads = feats // HD
    groups = lengths.shape[0]
    token_count = groups * BEAMS
    all_rows = token_count * steps
    slots_local = cache_keys.shape[1]
    halves = gate_w.shape[0]
    half_width = gate_w.shape[2]
    width = kv_count * feats
    payload = feats + 2 * HD + LANES

    packed = pl.pallas_call(
        pack_kernel,
        out_shape=jax.ShapeDtypeStruct((wide_count, rows, payload), BF16),
        in_specs=[VMEM] * 3,
        out_specs=VMEM,
        name="pack",
    )(queries, new_kv, routes)
    gathered = sent(packed, "wide").reshape(all_rows, payload)

    slot_ids = wide_index * slots_local + jnp.arange(slots_local, dtype=jnp.int32)
    slot_hits = page_table[None, :, :] == slot_ids[:, None, None]
    group_ids = jnp.arange(groups, dtype=jnp.int32)
    block_starts = jnp.arange(page_table.shape[1], dtype=jnp.int32) * BLK
    owner_group = jnp.sum(jnp.where(slot_hits, group_ids[None, :, None], 0), axis=(1, 2))
    block_limit = jnp.sum(
        jnp.where(slot_hits, lengths[None, :, None] - block_starts[None, None, :], 0), axis=(1, 2)
    )
    own_tokens = wide_index * step_tok + jnp.arange(step_tok, dtype=jnp.int32)
    mask = chain_mask(parents, own_tokens, steps)
    mask = jnp.swapaxes(mask, 2, 3).reshape(rows, all_rows)

    sums = pl.pallas_call(
        attend_kernel,
        out_shape=jax.ShapeDtypeStruct((all_rows, feats + LANES), BF16),
        in_specs=[SMEM, SMEM, VMEM, VMEM, VMEM],
        out_specs=VMEM,
        scratch_shapes=[
            pltpu.VMEM((groups, BEAMS * steps * heads, HD), BF16),
            pltpu.VMEM((groups, BEAMS * steps * heads, 2 * HD), F32),
        ],
        compiler_params=pltpu.CompilerParams(vmem_limit_bytes=32 * MIB),
        name="attend",
    )(owner_group, block_limit, gathered, cache_keys[0], cache_values[0])
    gain = norm_gain.reshape(1, width)
    sums, gain = lax.optimization_barrier((sums, gain))
    arrived = sent(sums.reshape(wide_count, rows, feats + LANES), "wide")
    tail_num, tail_den = pl.pallas_call(
        suffix_kernel,
        out_shape=[jax.ShapeDtypeStruct((rows, feats), F32)] * 2,
        in_specs=[VMEM] * 3,
        out_specs=[VMEM] * 2,
        cost_estimate=pl.CostEstimate(flops=40_000_000, bytes_accessed=2_000_000, transcendentals=0),
        name="suffix",
    )(queries, gathered, mask)
    residual, copies = pl.pallas_call(
        residual_kernel,
        out_shape=[
            jax.ShapeDtypeStruct((rows, feats), BF16),
            jax.ShapeDtypeStruct((kv_count * wide_count, rows, feats), BF16),
        ],
        in_specs=[VMEM] * 4,
        out_specs=[VMEM] * 2,
        name="residual",
    )(arrived, tail_num, tail_den, stream_in)

    spread_rows = sent(copies, ("kv", "wide")).reshape(kv_count, all_rows, feats)
    per_unit = 2 if halves % 2 == 0 else 1
    units = halves // per_unit
    unit_width = per_unit * half_width
    gate_rows = jnp.swapaxes(gate_w, 1, 2).reshape(units, unit_width, width)
    up_rows = jnp.swapaxes(up_w, 1, 2).reshape(units, unit_width, width)
    down_rows = down_w.reshape(units, unit_width, width)
    partial = pl.pallas_call(
        functools.partial(expert_kernel, per_unit),
        out_shape=jax.ShapeDtypeStruct((kv_count, all_rows, feats), BF16),
        in_specs=[SMEM, VMEM, VMEM, VMEM, VMEM, HBM, HBM, HBM],
        out_specs=VMEM,
        scratch_shapes=[
            pltpu.VMEM((3 * units, unit_width, width), BF16),
            pltpu.VMEM((all_rows, width), BF16),
            pltpu.VMEM((LANES, all_rows), F32),
            pltpu.VMEM((units, unit_width, all_rows), BF16),
            pltpu.VMEM((kv_count, all_rows, feats), F32),
            pltpu.SemaphoreType.DMA((3 * units,)),
        ],
        compiler_params=pltpu.CompilerParams(vmem_limit_bytes=56 * MIB),
        cost_estimate=pl.CostEstimate(
            flops=6 * all_rows * halves * half_width * width,
            bytes_accessed=6 * halves * half_width * width,
            transcendentals=0,
        ),
        name="experts",
    )(
        (wide_index * halves).astype(jnp.int32).reshape(1),
        spread_rows,
        gathered,
        gain,
        router.T,
        gate_rows,
        up_rows,
        down_rows,
    )
    returned = sent(partial.reshape(kv_count * wide_count, rows, feats), ("kv", "wide"))
    moe_part = jnp.sum(returned.astype(F32), axis=0)
    out = (residual.astype(F32) + moe_part).astype(BF16)
    return out.reshape(step_tok, steps, feats)


def solution(mesh):
    return jax.shard_map(
        local,
        mesh=mesh,
        in_specs=(
            P("wide", None, "kv"),
            P("wide", None, "kv"),
            P("wide", None, None, "kv"),
            P("kv", "wide", None, None),
            P("kv", "wide", None, None),
            P(),
            P(),
            P(),
            P("wide", None, None),
            P(),
            P(),
            P("wide", None, "kv"),
            P("wide", None, "kv"),
            P("wide", "kv", None),
        ),
        out_specs=P("wide", None, "kv"),
        check_vma=False,
    )
```

```python
import functools
import math

import jax
import jax.numpy as jnp
from jax import lax
from jax.experimental import pallas as pl
from jax.experimental.pallas import tpu as pltpu
from jax.sharding import Mesh
from jax.sharding import PartitionSpec as P

HD = 128
E = 64
BEAMS = 8
BLK = 128
LANES = 128
MIB = 2**20
AHEAD = 6
F32 = jnp.float32
BF16 = jnp.bfloat16
NT = (((1,), (1,)), ((), ()))
TN = (((0,), (0,)), ((), ()))
VMEM = pl.BlockSpec(memory_space=pltpu.VMEM)
SMEM = pl.BlockSpec(memory_space=pltpu.SMEM)
HBM = pl.BlockSpec(memory_space=pltpu.HBM)
ANY = pl.BlockSpec(memory_space=pl.ANY)
WIDE = ("z", "core")


def small(shape, dtype):
    return math.prod(shape) * jnp.dtype(dtype).itemsize <= MIB


def near(array):
    if small(array.shape, array.dtype):
        return pltpu.with_memory_space_constraint(array, pltpu.VMEM)
    return array


def far(array):
    return pltpu.with_memory_space_constraint(array, pltpu.HBM)


def result(shape, dtype):
    if small(shape, dtype):
        return pltpu.VMEM(shape, dtype)
    return jax.ShapeDtypeStruct(shape, dtype)


def sent(block, axes):
    return lax.all_to_all(block, axes, split_axis=0, concat_axis=0, tiled=True)


def pack_kernel(query_ref, new_ref, route_ref, out_ref):
    step_tok, steps, feats = query_ref.shape
    lanes = lax.broadcasted_iota(jnp.int32, (steps, LANES), 1)
    parts = []
    for t in range(step_tok):
        named = route_ref[t]
        chosen = jnp.zeros((steps, LANES), F32)
        for i in range(named.shape[1]):
            chosen = jnp.where(named[:, i : i + 1] == lanes, 1.0, chosen)
        parts.append(
            jnp.concatenate(
                [
                    query_ref[t].astype(F32),
                    new_ref[t, :, 0, :].astype(F32),
                    new_ref[t, :, 1, :].astype(F32),
                    chosen,
                ],
                axis=1,
            )
        )
    block = jnp.concatenate(parts, axis=0).astype(BF16)
    for w in range(out_ref.shape[0]):
        out_ref[w] = block


def stage_kernel(
    table_ref, length_ref, key_hbm, value_hbm, router_hbm, gain_hbm, after_ref,
    key_ref, extended_ref, router_ref, gain_ref, valid_ref, sems,
):
    del after_ref
    slots = key_ref.shape[0]
    groups, blocks = table_ref.shape
    copies = [
        pltpu.make_async_copy(key_hbm, key_ref, sems.at[0]),
        pltpu.make_async_copy(value_hbm, extended_ref.at[:, :, pl.ds(0, HD)], sems.at[1]),
        pltpu.make_async_copy(router_hbm, router_ref, sems.at[2]),
        pltpu.make_async_copy(gain_hbm, gain_ref, sems.at[3]),
    ]
    for copy in copies:
        copy.start()
    extended_ref[:, :, HD:] = jnp.ones((slots, BLK, HD), BF16)
    valid_ref[...] = jnp.zeros_like(valid_ref)
    first_slot = lax.axis_index(WIDE) * slots
    place = lax.broadcasted_iota(jnp.int32, (1, BLK), 1)

    def look(i, carry):
        group, block = i // blocks, i % blocks
        slot = table_ref[group, block] - first_slot

        @pl.when((slot >= 0) & (slot < slots))
        def _():
            limit = length_ref[group] - block * BLK
            valid_ref[group, pl.ds(slot, 1), :] = jnp.where(place < limit, 1.0, 0.0)

        return carry

    lax.fori_loop(0, groups * blocks, look, 0)
    for copy in copies:
        copy.wait()


def attend_kernel(rows_ref, key_ref, extended_ref, valid_ref, out_ref, query_ref, weight_ref):
    slots = key_ref.shape[0]
    groups = valid_ref.shape[0]
    stacked = query_ref.shape[0]
    feats = out_ref.shape[1] - LANES
    heads = feats // HD
    span = stacked // heads
    scale = 1.0 / math.sqrt(HD)
    lanes = lax.broadcasted_iota(jnp.int32, (span, LANES), 1)

    def one_group(g, carry):
        rows = pl.ds(pl.multiple_of(g * span, span), span)
        for h in range(heads):
            query_ref[h * span : (h + 1) * span, :] = rows_ref[rows, h * HD : (h + 1) * HD]
        query = query_ref[...]
        for n in range(slots):
            scores = lax.dot_general(query, key_ref[n], NT, preferred_element_type=F32)
            weights = jnp.where(valid_ref[g, n : n + 1, :] > 0, jnp.exp(scores * scale), 0.0)
            weight_ref[:, n * BLK : (n + 1) * BLK] = weights.astype(BF16)
        sums = jnp.dot(
            weight_ref[...],
            extended_ref[...].reshape(slots * BLK, 2 * HD),
            preferred_element_type=F32,
        )
        tail = jnp.zeros((span, LANES), F32)
        for h in range(heads):
            piece = sums[h * span : (h + 1) * span, :]
            out_ref[rows, h * HD : (h + 1) * HD] = piece[:, :HD].astype(BF16)
            high = piece[:, HD:].astype(BF16).astype(F32)
            tail = jnp.where(lanes == h, high, tail)
            tail = jnp.where(lanes == heads + h, piece[:, HD:] - high, tail)
        out_ref[rows, feats:] = tail.astype(BF16)
        return carry

    lax.fori_loop(0, groups, one_group, 0, unroll=groups <= 2)


def suffix_kernel(parent_ref, query_ref, rows_ref, stream_ref, num_ref, den_ref, own_ref):
    step_tok, steps, feats = query_ref.shape
    rows = step_tok * steps
    heads = feats // HD
    scale = 1.0 / math.sqrt(HD)
    own = jnp.concatenate([query_ref[t].astype(F32) for t in range(step_tok)], axis=0)
    own_ref[...] = jnp.concatenate([stream_ref[t].astype(F32) for t in range(step_tok)], axis=0)
    stacked = jnp.concatenate([own[:, h * HD : (h + 1) * HD] for h in range(heads)], axis=0)
    keys = rows_ref[:, feats : feats + HD]
    values = rows_ref[:, feats + HD : feats + 2 * HD]
    scores = lax.dot_general(stacked.astype(BF16), keys, NT, preferred_element_type=F32)
    first_token = lax.axis_index(WIDE) * step_tok
    shape = (heads * rows, rows_ref.shape[0])
    row = lax.broadcasted_iota(jnp.int32, shape, 0) % rows
    column = lax.broadcasted_iota(jnp.int32, shape, 1)
    mask = jnp.zeros(shape, F32)
    for t in range(step_tok):
        token = first_token + t
        base = token // BEAMS * BEAMS
        for s in range(steps):
            ancestor = token
            for j in range(s, -1, -1):
                hit = (row == t * steps + s) & (column == ancestor * steps + j)
                mask = jnp.where(hit, 1.0, mask)
                if j > 0:
                    ancestor = base + parent_ref[j - 1, ancestor]
    weights = jnp.where(mask > 0, jnp.exp(scores * scale), 0.0).astype(BF16)
    extended = jnp.concatenate([values, jnp.ones_like(values)], axis=1)
    sums = jnp.dot(weights, extended, preferred_element_type=F32)
    for h in range(heads):
        num_ref[:, h * HD : (h + 1) * HD] = sums[h * rows : (h + 1) * rows, :HD]
        den_ref[:, h * HD : (h + 1) * HD] = sums[h * rows : (h + 1) * rows, HD:]


def residual_kernel(sums_ref, num_ref, den_ref, stream_ref, out_ref, spread_ref):
    rows, feats = out_ref.shape
    heads = feats // HD
    total = sums_ref[0].astype(F32)
    for w in range(1, sums_ref.shape[0]):
        total = total + sums_ref[w].astype(F32)
    dens = total[:, feats : feats + heads] + total[:, feats + heads : feats + 2 * heads]
    parts = []
    for h in range(heads):
        at = slice(h * HD, (h + 1) * HD)
        attended = (total[:, at] + num_ref[:, at]) / (dens[:, h : h + 1] + den_ref[:, at])
        parts.append(stream_ref[:, at] + attended.astype(BF16).astype(F32))
    residual = jnp.concatenate(parts, axis=1).astype(BF16)
    out_ref[...] = residual
    for d in range(spread_ref.shape[0]):
        spread_ref[d] = residual


def expert_kernel(
    per_unit, own_ref, other_ref, chosen_ref, gain_ref, router_ref, gate_hbm, up_hbm, down_hbm,
    mine_ref, theirs_ref, slot_ref, norm_ref, share_ref, hidden_ref, total_ref, sems,
):
    kv_count, count, feats = total_ref.shape
    pieces, rows, _ = own_ref.shape
    chips = pieces // kv_count
    core = lax.axis_index("core")
    units, width, _ = gate_hbm.shape
    sources = [ref.at[l] for l in range(units) for ref in (gate_hbm, up_hbm)]
    sources += [down_hbm.at[l] for l in range(units)]
    copies = [
        pltpu.make_async_copy(source, slot_ref.at[i], sems.at[i])
        for i, source in enumerate(sources)
    ]
    for copy in copies[:AHEAD]:
        copy.start()

    def arrive(i):
        copies[i].wait()
        if i + AHEAD < len(copies):
            copies[i + AHEAD].start()

    def place(z, carry):
        for ref, side in ((own_ref, core), (other_ref, 1 - core)):
            at = pl.ds(pl.multiple_of((z * 2 + side) * rows, rows), rows)
            for k in range(kv_count):
                total_ref[k, at, :] = ref[k * chips + z].astype(F32)
        return carry

    lax.fori_loop(0, chips, place, 0, unroll=chips <= 8)
    block = 64
    offset = chosen_ref.shape[1] - LANES
    for b in range(count // block):
        at = slice(b * block, (b + 1) * block)
        squares = jnp.zeros((block, 1), F32)
        for k in range(kv_count):
            part = total_ref[k, at, :]
            squares += jnp.sum(part * part, axis=1, keepdims=True)
        root = lax.rsqrt(squares / (kv_count * feats) + 1e-06)
        for k in range(kv_count):
            columns = slice(k * feats, (k + 1) * feats)
            part = total_ref[k, at, :]
            norm_ref[at, columns] = (part * root * gain_ref[columns].reshape(1, feats)).astype(BF16)
        logits = lax.dot_general(norm_ref[at, :], router_ref[...], NT, preferred_element_type=F32)
        chosen = chosen_ref[at, offset:].astype(F32)
        raised = jnp.where(chosen[:, :E] > 0, jnp.exp(logits), 0.0)
        share = raised / jnp.sum(raised, axis=1, keepdims=True)
        share = jnp.concatenate([share, jnp.zeros((block, LANES - E), F32)], axis=1)
        share_ref[:, at] = share.T
    normed = norm_ref[...]
    first_half = lax.axis_index(WIDE) * units * per_unit
    for l in range(units):
        arrive(2 * l)
        arrive(2 * l + 1)
        gate = lax.dot_general(slot_ref[2 * l], normed, NT, preferred_element_type=F32)
        up = lax.dot_general(slot_ref[2 * l + 1], normed, NT, preferred_element_type=F32)
        weight = share_ref[pl.ds((first_half + l * per_unit) // 2, 1), :]
        hidden_ref[l] = (gate / (1.0 + jnp.exp(-gate)) * up * weight).astype(BF16)
    for l in range(units):
        i = 2 * units + l
        arrive(i)
        for k in range(kv_count):
            columns = slice(k * feats, (k + 1) * feats)
            piece = lax.dot_general(
                hidden_ref[l], slot_ref[i, :, columns], TN, preferred_element_type=F32
            )
            total_ref[k] = piece if l == 0 else piece + total_ref[k]

    def hand_out(z, carry):
        for ref, side in ((mine_ref, core), (theirs_ref, 1 - core)):
            at = pl.ds(pl.multiple_of((z * 2 + side) * rows, rows), rows)
            for k in range(kv_count):
                ref[k * chips + z] = total_ref[k, at, :].astype(BF16)
        return carry

    lax.fori_loop(0, chips, hand_out, 0, unroll=chips <= 8)


def add_kernel(left_ref, right_ref, out_ref):
    for i in range(out_ref.shape[0]):
        out_ref[i] = (left_ref[i].astype(F32) + right_ref[i].astype(F32)).astype(BF16)


def finish_kernel(parts_ref, residual_ref, out_ref):
    total = parts_ref[0].astype(F32)
    for i in range(1, parts_ref.shape[0]):
        total = total + parts_ref[i].astype(F32)
    total = (residual_ref[...].astype(F32) + total).astype(BF16)
    step_tok, steps, _ = out_ref.shape
    for t in range(step_tok):
        out_ref[t] = total[t * steps : (t + 1) * steps]


def local(
    stream_in,
    queries,
    new_kv,
    cache_keys,
    cache_values,
    lengths,
    page_table,
    parents,
    routes,
    norm_gain,
    router,
    gate_w,
    up_w,
    down_w,
):
    kv_count = lax.axis_size("kv")
    chips = lax.axis_size("z")
    wide_count = lax.axis_size(WIDE)
    step_tok, steps, feats = stream_in.shape
    rows = step_tok * steps
    heads = feats // HD
    groups = lengths.shape[0]
    all_rows = groups * BEAMS * steps
    slots = cache_keys.shape[1]
    halves = gate_w.shape[0]
    half_width = gate_w.shape[2]
    width = kv_count * feats
    payload = feats + 2 * HD + LANES

    packed = pl.pallas_call(
        pack_kernel,
        out_shape=result((wide_count, rows, payload), BF16),
        in_specs=[VMEM] * 3,
        out_specs=VMEM,
        name="pack",
    )(queries, new_kv, routes)
    gathered = near(sent(packed, WIDE).reshape(all_rows, payload))
    keys, extended, router_rows, gain, valid = pl.pallas_call(
        stage_kernel,
        out_shape=[
            result((slots, BLK, HD), BF16),
            result((slots, BLK, 2 * HD), BF16),
            result((E, width), BF16),
            result((width,), F32),
            result((groups, slots, BLK), F32),
        ],
        in_specs=[SMEM, SMEM, HBM, HBM, HBM, HBM, ANY],
        out_specs=[VMEM] * 5,
        scratch_shapes=[pltpu.SemaphoreType.DMA((4,))],
        compiler_params=pltpu.CompilerParams(vmem_limit_bytes=16 * MIB),
        name="stage",
    )(
        far(page_table),
        far(lengths),
        far(cache_keys[0]),
        far(cache_values[0]),
        far(router.T),
        far(norm_gain),
        packed,
    )
    sums = pl.pallas_call(
        attend_kernel,
        out_shape=result((all_rows, feats + LANES), BF16),
        in_specs=[VMEM] * 4,
        out_specs=VMEM,
        scratch_shapes=[
            pltpu.VMEM((BEAMS * steps * heads, HD), BF16),
            pltpu.VMEM((BEAMS * steps * heads, slots * BLK), BF16),
        ],
        compiler_params=pltpu.CompilerParams(vmem_limit_bytes=32 * MIB),
        name="attend",
    )(gathered, near(keys), near(extended), near(valid))
    arrived = sent(sums.reshape(wide_count, rows, feats + LANES), WIDE)
    tail_num, tail_den, stream = pl.pallas_call(
        suffix_kernel,
        out_shape=[result((rows, feats), F32)] * 3,
        in_specs=[SMEM, VMEM, VMEM, VMEM],
        out_specs=[VMEM] * 3,
        cost_estimate=pl.CostEstimate(flops=40_000_000, bytes_accessed=2_000_000, transcendentals=0),
        name="suffix",
    )(far(parents.T), far(queries), gathered, far(stream_in))
    residual, copies = pl.pallas_call(
        residual_kernel,
        out_shape=[
            result((rows, feats), BF16),
            result((kv_count * chips, rows, feats), BF16),
        ],
        in_specs=[VMEM] * 4,
        out_specs=[VMEM] * 2,
        compiler_params=pltpu.CompilerParams(vmem_limit_bytes=16 * MIB),
        name="residual",
    )(near(arrived), near(tail_num), near(tail_den), near(stream))

    own = sent(copies, ("kv", "z"))
    other = lax.ppermute(own, "core", ((0, 1), (1, 0)))
    per_unit = 2 if halves % 2 == 0 else 1
    units = halves // per_unit
    unit_width = per_unit * half_width
    mine, theirs = pl.pallas_call(
        functools.partial(expert_kernel, per_unit),
        out_shape=[result((kv_count * chips, rows, feats), BF16)] * 2,
        in_specs=[VMEM] * 5 + [HBM] * 3,
        out_specs=[VMEM] * 2,
        scratch_shapes=[
            pltpu.VMEM((3 * units, unit_width, width), BF16),
            pltpu.VMEM((all_rows, width), BF16),
            pltpu.VMEM((LANES, all_rows), F32),
            pltpu.VMEM((units, unit_width, all_rows), BF16),
            pltpu.VMEM((kv_count, all_rows, feats), F32),
            pltpu.SemaphoreType.DMA((3 * units,)),
        ],
        compiler_params=pltpu.CompilerParams(vmem_limit_bytes=56 * MIB),
        cost_estimate=pl.CostEstimate(
            flops=6 * all_rows * halves * half_width * width,
            bytes_accessed=6 * halves * half_width * width,
            transcendentals=0,
        ),
        name="experts",
    )(
        near(own),
        near(other),
        gathered,
        near(gain),
        near(router_rows),
        jnp.swapaxes(gate_w, 1, 2).reshape(units, unit_width, width),
        jnp.swapaxes(up_w, 1, 2).reshape(units, unit_width, width),
        down_w.reshape(units, unit_width, width),
    )
    swapped = lax.ppermute(theirs, "core", ((0, 1), (1, 0)))
    both = pl.pallas_call(
        add_kernel,
        out_shape=result(mine.shape, BF16),
        in_specs=[VMEM] * 2,
        out_specs=VMEM,
        name="add",
    )(near(mine), near(swapped))
    returned = sent(both, ("kv", "z"))
    return pl.pallas_call(
        finish_kernel,
        out_shape=jax.ShapeDtypeStruct(stream_in.shape, BF16),
        in_specs=[VMEM] * 2,
        out_specs=VMEM,
        name="finish",
    )(near(returned), near(residual))


def solution(mesh):
    kv_count, wide_count = mesh.devices.shape
    split = Mesh(mesh.devices.reshape(kv_count, wide_count // 2, 2), ("kv",) + WIDE)
    return jax.shard_map(
        local,
        mesh=split,
        in_specs=(
            P(WIDE, None, "kv"),
            P(WIDE, None, "kv"),
            P(WIDE, None, None, "kv"),
            P("kv", WIDE, None, None),
            P("kv", WIDE, None, None),
            P(),
            P(),
            P(),
            P(WIDE, None, None),
            P(),
            P(),
            P(WIDE, None, "kv"),
            P(WIDE, None, "kv"),
            P(WIDE, "kv", None),
        ),
        out_specs=P(WIDE, None, "kv"),
        check_vma=False,
    )
```

```python
import functools
import math

import jax
import jax.numpy as jnp
from jax import lax
from jax.experimental import pallas as pl
from jax.experimental.pallas import tpu as pltpu
from jax.sharding import Mesh
from jax.sharding import PartitionSpec as P

HD = 128
E = 64
BEAMS = 8
BLK = 128
LANES = 128
MIB = 2**20
AHEAD = 6
EARLY = (2, 2)
SHIFTS = (3, 1, 2)
F32 = jnp.float32
BF16 = jnp.bfloat16
NT = (((1,), (1,)), ((), ()))
TN = (((0,), (0,)), ((), ()))
VMEM = pl.BlockSpec(memory_space=pltpu.VMEM)
SMEM = pl.BlockSpec(memory_space=pltpu.SMEM)
HBM = pl.BlockSpec(memory_space=pltpu.HBM)
ANY = pl.BlockSpec(memory_space=pl.ANY)
WIDE = ("z", "core")


def small(shape, dtype):
    return math.prod(shape) * jnp.dtype(dtype).itemsize <= MIB


def near(array):
    if small(array.shape, array.dtype):
        return pltpu.with_memory_space_constraint(array, pltpu.VMEM)
    return array


def far(array):
    return pltpu.with_memory_space_constraint(array, pltpu.HBM)


def result(shape, dtype):
    if small(shape, dtype):
        return pltpu.VMEM(shape, dtype)
    return jax.ShapeDtypeStruct(shape, dtype)


def sent(block, axes):
    return lax.all_to_all(block, axes, split_axis=0, concat_axis=0, tiled=True)


def pack_kernel(query_ref, new_ref, route_ref, out_ref):
    step_tok, steps, feats = query_ref.shape
    lanes = lax.broadcasted_iota(jnp.int32, (steps, LANES), 1)
    parts = []
    for t in range(step_tok):
        named = route_ref[t]
        chosen = jnp.zeros((steps, LANES), F32)
        for i in range(named.shape[1]):
            chosen = jnp.where(named[:, i : i + 1] == lanes, 1.0, chosen)
        parts.append(
            jnp.concatenate(
                [
                    query_ref[t].astype(F32),
                    new_ref[t, :, 0, :].astype(F32),
                    new_ref[t, :, 1, :].astype(F32),
                    chosen,
                ],
                axis=1,
            )
        )
    block = jnp.concatenate(parts, axis=0).astype(BF16)
    if len(out_ref.shape) == 2:
        out_ref[...] = block
    else:
        for w in range(out_ref.shape[0]):
            out_ref[w] = block


def stage_kernel(
    table_ref, length_ref, parent_ref, key_hbm, value_hbm, router_hbm, gain_hbm, query_ref,
    stream_ref, after_ref,
    key_ref, extended_ref, router_ref, gain_ref, valid_ref, own_ref, own_stream_ref, mask_ref, sems,
):
    del after_ref
    slots = key_ref.shape[0]
    groups, blocks = table_ref.shape
    copies = [
        pltpu.make_async_copy(key_hbm, key_ref, sems.at[0]),
        pltpu.make_async_copy(value_hbm, extended_ref.at[:, :, pl.ds(0, HD)], sems.at[1]),
        pltpu.make_async_copy(router_hbm, router_ref, sems.at[2]),
        pltpu.make_async_copy(gain_hbm, gain_ref, sems.at[3]),
    ]
    for copy in copies:
        copy.start()
    extended_ref[:, :, HD:] = jnp.ones((slots, BLK, HD), BF16)
    valid_ref[...] = jnp.zeros_like(valid_ref)
    first_slot = lax.axis_index(WIDE) * slots
    place = lax.broadcasted_iota(jnp.int32, (1, BLK), 1)

    def look(i, carry):
        group, block = i // blocks, i % blocks
        slot = table_ref[group, block] - first_slot

        @pl.when((slot >= 0) & (slot < slots))
        def _():
            limit = length_ref[group] - block * BLK
            valid_ref[group, pl.ds(slot, 1), :] = jnp.where(place < limit, 1.0, 0.0)

        return carry

    lax.fori_loop(0, groups * blocks, look, 0)
    step_tok, steps, feats = query_ref.shape
    rows = step_tok * steps
    heads = feats // HD
    own = jnp.concatenate([query_ref[t].astype(F32) for t in range(step_tok)], axis=0)
    stacked = jnp.concatenate([own[:, h * HD : (h + 1) * HD] for h in range(heads)], axis=0)
    own_ref[...] = stacked.astype(BF16)
    own_stream_ref[...] = jnp.concatenate(
        [stream_ref[t].astype(F32) for t in range(step_tok)], axis=0
    )
    first_token = lax.axis_index(WIDE) * step_tok
    row = lax.broadcasted_iota(jnp.int32, mask_ref.shape, 0) % rows
    column = lax.broadcasted_iota(jnp.int32, mask_ref.shape, 1)
    mask = jnp.zeros(mask_ref.shape, F32)
    for t in range(step_tok):
        token = first_token + t
        base = token // BEAMS * BEAMS
        for s in range(steps):
            ancestor = token
            for j in range(s, -1, -1):
                hit = (row == t * steps + s) & (column == ancestor * steps + j)
                mask = jnp.where(hit, 1.0, mask)
                if j > 0:
                    ancestor = base + parent_ref[j - 1, ancestor]
    mask_ref[...] = mask
    for copy in copies:
        copy.wait()


def attend_kernel(part_count, early_count, *refs):
    part_refs, refs = refs[:part_count], refs[part_count:]
    key_ref, extended_ref, valid_ref, own_ref, mask_ref, gate_hbm, up_hbm = refs[:7]
    out_ref, chosen_ref = refs[7:9]
    refs = refs[9:]
    early_copies = []
    if early_count:
        early_ref, early_sem = refs[0], refs[-1]
        refs = refs[1:]
        early_copies = [
            pltpu.make_async_copy((gate_hbm, up_hbm)[i % 2].at[i // 2], early_ref.at[i], early_sem.at[i])
            for i in range(early_count)
        ]
    for copy in early_copies:
        copy.start()
    query_ref, weight_ref, total_ref, rows_ref = refs[:4]
    if part_count == 1:
        for w in range(part_refs[0].shape[0]):
            count = part_refs[0].shape[1]
            rows_ref[w * count : (w + 1) * count, :] = part_refs[0][w].astype(F32)
    else:
        chip, core = lax.axis_index("z"), lax.axis_index("core")
        for k, ref in enumerate(part_refs):
            count = ref.shape[1]
            source = (chip + part_count - k) % part_count
            for i in range(2):
                side = core if i == 0 else 1 - core
                at = pl.ds(pl.multiple_of((source * 2 + side) * count, count), count)
                rows_ref[at, :] = ref[i].astype(F32)
    slots = key_ref.shape[0]
    groups = valid_ref.shape[0]
    stacked = query_ref.shape[0]
    feats = out_ref.shape[1] - LANES
    heads = feats // HD
    span = stacked // heads
    scale = 1.0 / math.sqrt(HD)

    def one_group(g, carry):
        rows = pl.ds(pl.multiple_of(g * span, span), span)
        for h in range(heads):
            query_ref[h * span : (h + 1) * span, :] = rows_ref[
                rows, h * HD : (h + 1) * HD
            ].astype(BF16)
        query = query_ref[...]
        for n in range(slots):
            scores = lax.dot_general(query, key_ref[n], NT, preferred_element_type=F32)
            weights = jnp.where(valid_ref[g, n : n + 1, :] > 0, jnp.exp(scores * scale), 0.0)
            weight_ref[:, n * BLK : (n + 1) * BLK] = weights.astype(BF16)
        sums = jnp.dot(
            weight_ref[...],
            extended_ref[...].reshape(slots * BLK, 2 * HD),
            preferred_element_type=F32,
        )
        for h in range(heads):
            total_ref[h, rows, :] = sums[h * span : (h + 1) * span, :]
        return carry

    lax.fori_loop(0, groups, one_group, 0, unroll=groups <= 2)
    chosen_ref[...] = rows_ref[:, feats + 2 * HD :]
    keys = rows_ref[:, feats : feats + HD].astype(BF16)
    values = rows_ref[:, feats + HD : feats + 2 * HD].astype(BF16)
    scores = lax.dot_general(own_ref[...], keys, NT, preferred_element_type=F32)
    weights = jnp.where(mask_ref[...] > 0, jnp.exp(scores * scale), 0.0).astype(BF16)
    extended = jnp.concatenate([values, jnp.ones_like(values)], axis=1)
    tail = jnp.dot(weights, extended, preferred_element_type=F32)
    rows = own_ref.shape[0] // heads
    mine = pl.ds(pl.multiple_of(lax.axis_index(WIDE) * rows, rows), rows)
    for h in range(heads):
        total_ref[h, mine, :] += tail[h * rows : (h + 1) * rows, :]
    lanes = lax.broadcasted_iota(jnp.int32, (span, LANES), 1)

    def pack_group(g, carry):
        rows = pl.ds(pl.multiple_of(g * span, span), span)
        last = jnp.zeros((span, LANES), F32)
        for h in range(heads):
            piece = total_ref[h, rows, :]
            out_ref[rows, h * HD : (h + 1) * HD] = piece[:, :HD].astype(BF16)
            high = piece[:, HD:].astype(BF16).astype(F32)
            last = jnp.where(lanes == h, high, last)
            last = jnp.where(lanes == heads + h, piece[:, HD:] - high, last)
        out_ref[rows, feats:] = last.astype(BF16)
        return carry

    lax.fori_loop(0, groups, pack_group, 0, unroll=groups <= 2)
    for copy in early_copies:
        copy.wait()


def normalise(side, pieces_ref, chosen_ref, gain_ref, router_ref, stack_ref, pick_ref, norm_ref, share_ref):
    kv_count, count, feats = stack_ref.shape
    pieces, rows, _ = pieces_ref.shape
    chips = pieces // kv_count

    def place(z, carry):
        to = pl.ds(pl.multiple_of(z * rows, rows), rows)
        source = pl.ds(pl.multiple_of((z * 2 + side) * rows, rows), rows)
        pick_ref[to, :] = chosen_ref[source, :]
        for k in range(kv_count):
            stack_ref[k, to, :] = pieces_ref[k * chips + z].astype(F32)
        return carry

    lax.fori_loop(0, chips, place, 0, unroll=chips <= 8)
    block = min(64, count)
    for b in range(count // block):
        at = slice(b * block, (b + 1) * block)
        squares = jnp.zeros((block, 1), F32)
        for k in range(kv_count):
            part = stack_ref[k, at, :]
            squares += jnp.sum(part * part, axis=1, keepdims=True)
        root = lax.rsqrt(squares / (kv_count * feats) + 1e-06)
        for k in range(kv_count):
            columns = slice(k * feats, (k + 1) * feats)
            part = stack_ref[k, at, :]
            norm_ref[at, columns] = (part * root * gain_ref[columns].reshape(1, feats)).astype(BF16)
        logits = lax.dot_general(norm_ref[at, :], router_ref[...], NT, preferred_element_type=F32)
        raised = jnp.where(pick_ref[at, :E] > 0, jnp.exp(logits), 0.0)
        share = raised / jnp.sum(raised, axis=1, keepdims=True)
        share = jnp.concatenate([share, jnp.zeros((block, LANES - E), F32)], axis=1)
        share_ref[:, at] = share.T


def fetch_kernel(skip, count, pieces_ref, chosen_ref, gain_ref, router_ref, gate_hbm, up_hbm, *refs):
    norm_ref, share_ref = refs[:2]
    copies = [
        pltpu.make_async_copy(
            (gate_hbm, up_hbm)[(i + skip) % 2].at[(i + skip) // 2], refs[2].at[i], refs[-1].at[i]
        )
        for i in range(count)
    ]
    for copy in copies:
        copy.start()
    stack_ref, pick_ref = refs[-3:-1]
    normalise(
        lax.axis_index("core"),
        pieces_ref, chosen_ref, gain_ref, router_ref, stack_ref, pick_ref, norm_ref, share_ref,
    )
    for copy in copies:
        copy.wait()


def residual_kernel(sums_ref, stream_ref, out_ref, spread_ref):
    rows, feats = out_ref.shape
    heads = feats // HD
    total = sums_ref[0].astype(F32)
    for w in range(1, sums_ref.shape[0]):
        total = total + sums_ref[w].astype(F32)
    dens = total[:, feats : feats + heads] + total[:, feats + heads : feats + 2 * heads]
    parts = []
    for h in range(heads):
        at = slice(h * HD, (h + 1) * HD)
        attended = total[:, at] / dens[:, h : h + 1]
        parts.append(stream_ref[:, at] + attended.astype(BF16).astype(F32))
    residual = jnp.concatenate(parts, axis=1).astype(BF16)
    out_ref[...] = residual
    for d in range(spread_ref.shape[0]):
        spread_ref[d] = residual


def expert_kernel(
    per_unit, early_count, pieces_ref, norm_own_ref, share_own_ref, chosen_ref, gain_ref, router_ref,
    gate_hbm, up_hbm, down_hbm, *refs,
):
    early_refs = refs[: len(early_count)]
    mine_ref, theirs_ref, slot_ref, stack_ref, pick_ref, norm_ref, half_ref, share_ref = refs[
        len(early_count) : len(early_count) + 8
    ]
    hidden_ref, total_ref, sems = refs[len(early_count) + 8 :]
    kv_count, both, feats = total_ref.shape
    count = both // 2
    pieces, rows, _ = pieces_ref.shape
    chips = pieces // kv_count
    units, width, _ = gate_hbm.shape
    sources = [ref.at[l] for l in range(units) for ref in (gate_hbm, up_hbm)]
    sources += [down_hbm.at[l] for l in range(units)]
    blocks = [ref.at[i] for ref in early_refs for i in range(ref.shape[0])]
    early = len(blocks)
    blocks += [slot_ref.at[i] for i in range(len(sources) - early)]
    copies = [
        pltpu.make_async_copy(sources[i], blocks[i], sems.at[i - early])
        for i in range(early, len(sources))
    ]
    for copy in copies[:AHEAD]:
        copy.start()

    def arrive(i):
        if i >= early:
            copies[i - early].wait()
            if i - early + AHEAD < len(copies):
                copies[i - early + AHEAD].start()

    normalise(
        1 - lax.axis_index("core"),
        pieces_ref, chosen_ref, gain_ref, router_ref, stack_ref, pick_ref, norm_ref, half_ref,
    )
    share_ref[:, :count] = share_own_ref[...]
    share_ref[:, count:] = half_ref[...]
    normed = jnp.concatenate([norm_own_ref[...], norm_ref[...]], axis=0)
    first_half = lax.axis_index(WIDE) * units * per_unit
    for l in range(units):
        arrive(2 * l)
        arrive(2 * l + 1)
        gate = lax.dot_general(blocks[2 * l][...], normed, NT, preferred_element_type=F32)
        up = lax.dot_general(blocks[2 * l + 1][...], normed, NT, preferred_element_type=F32)
        weight = share_ref[pl.ds((first_half + l * per_unit) // 2, 1), :]
        hidden_ref[l] = (gate / (1.0 + jnp.exp(-gate)) * up * weight).astype(BF16)
    for l in range(units):
        i = 2 * units + l
        arrive(i)
        for k in range(kv_count):
            columns = slice(k * feats, (k + 1) * feats)
            piece = lax.dot_general(
                hidden_ref[l], blocks[i][:, columns], TN, preferred_element_type=F32
            )
            total_ref[k] = piece if l == 0 else piece + total_ref[k]

    def hand_out(z, carry):
        for ref, start in ((mine_ref, 0), (theirs_ref, count)):
            at = pl.ds(pl.multiple_of(start + z * rows, rows), rows)
            for k in range(kv_count):
                ref[k * chips + z] = total_ref[k, at, :].astype(BF16)
        return carry

    lax.fori_loop(0, chips, hand_out, 0, unroll=chips <= 8)


def add_kernel(left_ref, right_ref, out_ref):
    for i in range(out_ref.shape[0]):
        out_ref[i] = (left_ref[i].astype(F32) + right_ref[i].astype(F32)).astype(BF16)


def finish_kernel(parts_ref, residual_ref, out_ref):
    total = parts_ref[0].astype(F32)
    for i in range(1, parts_ref.shape[0]):
        total = total + parts_ref[i].astype(F32)
    total = (residual_ref[...].astype(F32) + total).astype(BF16)
    step_tok, steps, _ = out_ref.shape
    for t in range(step_tok):
        out_ref[t] = total[t * steps : (t + 1) * steps]


def local(
    stream_in,
    queries,
    new_kv,
    cache_keys,
    cache_values,
    lengths,
    page_table,
    parents,
    routes,
    norm_gain,
    router,
    gate_w,
    up_w,
    down_w,
):
    kv_count = lax.axis_size("kv")
    chips = lax.axis_size("z")
    wide_count = lax.axis_size(WIDE)
    step_tok, steps, feats = stream_in.shape
    rows = step_tok * steps
    heads = feats // HD
    groups = lengths.shape[0]
    all_rows = groups * BEAMS * steps
    slots = cache_keys.shape[1]
    halves = gate_w.shape[0]
    half_width = gate_w.shape[2]
    width = kv_count * feats
    payload = feats + 2 * HD + LANES

    packed = pl.pallas_call(
        pack_kernel,
        out_shape=result((rows, payload) if chips <= 4 else (wide_count, rows, payload), BF16),
        in_specs=[VMEM] * 3,
        out_specs=VMEM,
        name="pack",
    )(queries, new_kv, routes)
    if chips <= 4:
        pair = jnp.stack([packed, lax.ppermute(packed, "core", ((0, 1), (1, 0)))])
        parts = {0: pair}
        for k in SHIFTS:
            if k < chips:
                parts[k] = lax.ppermute(pair, "z", [(i, (i + k) % chips) for i in range(chips)])
        parts = [near(parts[k]) for k in range(chips)]
    else:
        parts = [sent(packed, WIDE)]
    per_unit = 2 if halves % 2 == 0 else 1
    units = halves // per_unit
    unit_width = per_unit * half_width
    gate_rows = far(jnp.swapaxes(gate_w, 1, 2).reshape(units, unit_width, width))
    up_rows = far(jnp.swapaxes(up_w, 1, 2).reshape(units, unit_width, width))
    down_rows = far(down_w.reshape(units, unit_width, width))
    early_count = EARLY if 2 * units >= sum(EARLY) else ()

    keys, extended, router_rows, gain, valid, own_rows, stream, mask = pl.pallas_call(
        stage_kernel,
        out_shape=[
            result((slots, BLK, HD), BF16),
            result((slots, BLK, 2 * HD), BF16),
            result((E, width), BF16),
            result((width,), F32),
            result((groups, slots, BLK), F32),
            result((heads * rows, HD), BF16),
            result((rows, feats), F32),
            result((heads * rows, all_rows), F32),
        ],
        in_specs=[SMEM] * 3 + [HBM] * 4 + [VMEM] * 2 + [ANY],
        out_specs=[VMEM] * 8,
        scratch_shapes=[pltpu.SemaphoreType.DMA((4,))],
        compiler_params=pltpu.CompilerParams(vmem_limit_bytes=16 * MIB),
        name="stage",
    )(
        far(page_table),
        far(lengths),
        far(parents.T),
        far(cache_keys[0]),
        far(cache_values[0]),
        far(router.T),
        far(norm_gain),
        far(queries),
        far(stream_in),
        packed,
    )
    early_shapes = [pltpu.VMEM((n, unit_width, width), BF16) for n in early_count]
    sums, chosen, *early = pl.pallas_call(
        functools.partial(attend_kernel, len(parts), early_count[0] if early_count else 0),
        out_shape=[
            result((all_rows, feats + LANES), BF16),
            result((all_rows, LANES), F32),
            *early_shapes[:1],
        ],
        in_specs=[VMEM] * (len(parts) + 5) + [HBM] * 2,
        out_specs=[VMEM] * (2 + len(early_shapes[:1])),
        scratch_shapes=[
            pltpu.VMEM((BEAMS * steps * heads, HD), BF16),
            pltpu.VMEM((BEAMS * steps * heads, slots * BLK), BF16),
            pltpu.VMEM((heads, all_rows, 2 * HD), F32),
            pltpu.VMEM((all_rows, payload), F32),
            pltpu.SemaphoreType.DMA((max(early_count[:1], default=1),)),
        ],
        compiler_params=pltpu.CompilerParams(vmem_limit_bytes=32 * MIB),
        name="attend",
    )(
        *parts, near(keys), near(extended), near(valid), near(own_rows), near(mask),
        gate_rows, up_rows,
    )
    arrived = sent(sums.reshape(wide_count, rows, feats + LANES), WIDE)
    residual, copies = pl.pallas_call(
        residual_kernel,
        out_shape=[
            result((rows, feats), BF16),
            result((kv_count * chips, rows, feats), BF16),
        ],
        in_specs=[VMEM] * 2,
        out_specs=[VMEM] * 2,
        compiler_params=pltpu.CompilerParams(vmem_limit_bytes=8 * MIB),
        name="residual",
    )(near(arrived), near(stream))

    own = sent(copies, ("kv", "z"))
    other = lax.ppermute(own, "core", ((0, 1), (1, 0)))
    half = all_rows // 2
    norm_own, share_own, *more = pl.pallas_call(
        functools.partial(fetch_kernel, *(early_count or (0, 0))),
        out_shape=[result((half, width), BF16), result((LANES, half), F32), *early_shapes[1:]],
        in_specs=[VMEM] * 4 + [HBM] * 2,
        out_specs=[VMEM] * (2 + len(early_shapes[1:])),
        scratch_shapes=[
            pltpu.VMEM((kv_count, half, feats), F32),
            pltpu.VMEM((half, LANES), F32),
            pltpu.SemaphoreType.DMA((max(early_count[1:], default=1),)),
        ],
        compiler_params=pltpu.CompilerParams(vmem_limit_bytes=16 * MIB),
        name="fetch",
    )(near(own), near(chosen), near(gain), near(router_rows), gate_rows, up_rows)
    early = early + more
    mine, theirs = pl.pallas_call(
        functools.partial(expert_kernel, per_unit, early_count),
        out_shape=[result((kv_count * chips, rows, feats), BF16)] * 2,
        in_specs=[VMEM] * 6 + [HBM] * 3 + [VMEM] * len(early),
        out_specs=[VMEM] * 2,
        scratch_shapes=[
            pltpu.VMEM((3 * units - sum(early_count), unit_width, width), BF16),
            pltpu.VMEM((kv_count, half, feats), F32),
            pltpu.VMEM((half, LANES), F32),
            pltpu.VMEM((half, width), BF16),
            pltpu.VMEM((LANES, half), F32),
            pltpu.VMEM((LANES, all_rows), F32),
            pltpu.VMEM((units, unit_width, all_rows), BF16),
            pltpu.VMEM((kv_count, all_rows, feats), F32),
            pltpu.SemaphoreType.DMA((3 * units,)),
        ],
        compiler_params=pltpu.CompilerParams(vmem_limit_bytes=46 * MIB),
        cost_estimate=pl.CostEstimate(
            flops=6 * all_rows * halves * half_width * width,
            bytes_accessed=6 * halves * half_width * width,
            transcendentals=0,
        ),
        name="experts",
    )(
        near(other),
        near(norm_own),
        near(share_own),
        near(chosen),
        near(gain),
        near(router_rows),
        gate_rows,
        up_rows,
        down_rows,
        *[pltpu.with_memory_space_constraint(block, pltpu.VMEM) for block in early],
    )
    swapped = lax.ppermute(theirs, "core", ((0, 1), (1, 0)))
    both = pl.pallas_call(
        add_kernel,
        out_shape=result(mine.shape, BF16),
        in_specs=[VMEM] * 2,
        out_specs=VMEM,
        name="add",
    )(near(mine), near(swapped))
    returned = sent(both, ("kv", "z"))
    return pl.pallas_call(
        finish_kernel,
        out_shape=jax.ShapeDtypeStruct(stream_in.shape, BF16),
        in_specs=[VMEM] * 2,
        out_specs=VMEM,
        name="finish",
    )(near(returned), near(residual))


def solution(mesh):
    kv_count, wide_count = mesh.devices.shape
    split = Mesh(mesh.devices.reshape(kv_count, wide_count // 2, 2), ("kv",) + WIDE)
    return jax.shard_map(
        local,
        mesh=split,
        in_specs=(
            P(WIDE, None, "kv"),
            P(WIDE, None, "kv"),
            P(WIDE, None, None, "kv"),
            P("kv", WIDE, None, None),
            P("kv", WIDE, None, None),
            P(),
            P(),
            P(),
            P(WIDE, None, None),
            P(),
            P(),
            P(WIDE, None, "kv"),
            P(WIDE, None, "kv"),
            P(WIDE, "kv", None),
        ),
        out_specs=P(WIDE, None, "kv"),
        check_vma=False,
    )
```

```python
import functools
import math

import jax
import jax.numpy as jnp
from jax import lax
from jax.experimental import pallas as pl
from jax.experimental.pallas import tpu as pltpu
from jax.sharding import Mesh
from jax.sharding import PartitionSpec as P

HD = 128
E = 64
BEAMS = 8
BLK = 128
LANES = 128
MIB = 2**20
AHEAD = 6
EARLY = (0, 0, 1, 3, 1)
SHIFTS = (3, 1, 2)
F32 = jnp.float32
BF16 = jnp.bfloat16
NT = (((1,), (1,)), ((), ()))
TN = (((0,), (0,)), ((), ()))
VMEM = pl.BlockSpec(memory_space=pltpu.VMEM)
HBM = pl.BlockSpec(memory_space=pltpu.HBM)
ANY = pl.BlockSpec(memory_space=pl.ANY)
WIDE = ("z", "core")


def small(shape, dtype):
    return math.prod(shape) * jnp.dtype(dtype).itemsize <= MIB


def near(array):
    if small(array.shape, array.dtype):
        return pltpu.with_memory_space_constraint(array, pltpu.VMEM)
    return array


def far(array):
    return pltpu.with_memory_space_constraint(array, pltpu.HBM)


def pinned(array):
    return pltpu.with_memory_space_constraint(array, pltpu.VMEM)


def result(shape, dtype):
    if small(shape, dtype):
        return pltpu.VMEM(shape, dtype)
    return jax.ShapeDtypeStruct(shape, dtype)


def sent(block, axes):
    return lax.all_to_all(block, axes, split_axis=0, concat_axis=0, tiled=True)


def pack_kernel(query_ref, new_ref, route_ref, out_ref):
    step_tok, steps, feats = query_ref.shape
    lanes = lax.broadcasted_iota(jnp.int32, (steps, LANES), 1)
    parts = []
    for t in range(step_tok):
        named = route_ref[t]
        chosen = jnp.zeros((steps, LANES), F32)
        for i in range(named.shape[1]):
            chosen = jnp.where(named[:, i : i + 1] == lanes, 1.0, chosen)
        parts.append(
            jnp.concatenate(
                [
                    query_ref[t].astype(F32),
                    new_ref[t, :, 0, :].astype(F32),
                    new_ref[t, :, 1, :].astype(F32),
                    chosen,
                ],
                axis=1,
            )
        )
    block = jnp.concatenate(parts, axis=0).astype(BF16)
    if len(out_ref.shape) == 2:
        out_ref[...] = block
    else:
        for w in range(out_ref.shape[0]):
            out_ref[w] = block


def early_copies(skip, count, gate_hbm, up_hbm, early_ref, sems):
    return [
        pltpu.make_async_copy(
            (gate_hbm, up_hbm)[(i + skip) % 2].at[(i + skip) // 2], early_ref.at[i], sems.at[i]
        )
        for i in range(count)
    ]


def stage_kernel(
    skip, count, table_hbm, length_hbm, parent_hbm, key_hbm, value_hbm, router_hbm, gain_hbm,
    gate_hbm, up_hbm, query_hbm, stream_hbm, after_ref,
    key_ref, extended_ref, router_ref, gain_ref, valid_ref, own_ref, own_stream_ref, mask_ref, *refs,
):
    del after_ref
    table_ref, length_ref, parent_ref, query_ref, stream_ref, sems = refs[-7:-1]
    early = early_copies(skip, count, gate_hbm, up_hbm, refs[0], refs[-1])
    first = [
        pltpu.make_async_copy(table_hbm, table_ref, sems.at[4]),
        pltpu.make_async_copy(length_hbm, length_ref, sems.at[5]),
        pltpu.make_async_copy(parent_hbm, parent_ref, sems.at[6]),
        pltpu.make_async_copy(query_hbm, query_ref, sems.at[7]),
        pltpu.make_async_copy(stream_hbm, stream_ref, sems.at[8]),
    ]
    for copy in first:
        copy.start()
    slots = key_ref.shape[0]
    groups, blocks = table_ref.shape
    copies = [
        pltpu.make_async_copy(key_hbm, key_ref, sems.at[0]),
        pltpu.make_async_copy(value_hbm, extended_ref.at[:, :, pl.ds(0, HD)], sems.at[1]),
        pltpu.make_async_copy(router_hbm, router_ref, sems.at[2]),
        pltpu.make_async_copy(gain_hbm, gain_ref, sems.at[3]),
    ]
    for copy in copies + early:
        copy.start()
    extended_ref[:, :, HD:] = jnp.ones((slots, BLK, HD), BF16)
    valid_ref[...] = jnp.zeros_like(valid_ref)
    for copy in first:
        copy.wait()
    first_slot = lax.axis_index(WIDE) * slots
    place = lax.broadcasted_iota(jnp.int32, (1, BLK), 1)

    def look_group(group, carry):
        length = length_ref[group]

        def look(block, limit):
            slot = table_ref[group, block] - first_slot

            @pl.when((slot >= 0) & (slot < slots))
            def _():
                valid_ref[group, pl.ds(slot, 1), :] = jnp.where(place < limit, 1.0, 0.0)

            return limit - BLK

        lax.fori_loop(0, blocks, look, length, unroll=4)
        return carry

    lax.fori_loop(0, groups, look_group, 0, unroll=groups <= 2)
    step_tok, steps, feats = query_ref.shape
    rows = step_tok * steps
    heads = feats // HD
    own = jnp.concatenate([query_ref[t].astype(F32) for t in range(step_tok)], axis=0)
    stacked = jnp.concatenate([own[:, h * HD : (h + 1) * HD] for h in range(heads)], axis=0)
    own_ref[...] = stacked.astype(BF16)
    own_stream_ref[...] = jnp.concatenate(
        [stream_ref[t].astype(F32) for t in range(step_tok)], axis=0
    )
    first_token = lax.axis_index(WIDE) * step_tok
    row = jnp.concatenate([lax.broadcasted_iota(jnp.int32, (rows, mask_ref.shape[1]), 0)] * heads, axis=0)
    column = lax.broadcasted_iota(jnp.int32, mask_ref.shape, 1)
    mask = jnp.zeros(mask_ref.shape, F32)
    for t in range(step_tok):
        token = first_token + t
        base = token // BEAMS * BEAMS
        for s in range(steps):
            ancestor = token
            for j in range(s, -1, -1):
                hit = (row == t * steps + s) & (column == ancestor * steps + j)
                mask = jnp.where(hit, 1.0, mask)
                if j > 0:
                    ancestor = base + parent_ref[j - 1, ancestor]
    mask_ref[...] = mask
    for copy in copies + early:
        copy.wait()


def with_denominators(numerators, denominators):
    lanes = lax.broadcasted_iota(jnp.int32, (numerators[0].shape[0], LANES), 1)
    heads = len(numerators)
    last = jnp.zeros(lanes.shape, F32)
    for h, denominator in enumerate(denominators):
        high = denominator.astype(BF16).astype(F32)
        last = jnp.where(lanes == h, high, last)
        last = jnp.where(lanes == heads + h, denominator - high, last)
    return jnp.concatenate(numerators + [last], axis=1).astype(BF16)


def denominators_of(total, feats):
    heads = feats // HD
    return total[:, feats : feats + heads] + total[:, feats + heads : feats + 2 * heads]


def bring_kernel(skip, count, after_ref, gate_hbm, up_hbm, early_ref, sems):
    del after_ref
    copies = early_copies(skip, count, gate_hbm, up_hbm, early_ref, sems)
    for copy in copies:
        copy.start()
    for copy in copies:
        copy.wait()


def merge_kernel(held, left_ref, right_ref, *out_refs):
    out_refs = out_refs[held:]
    feats = left_ref.shape[2] - LANES
    for k, ref in enumerate(out_refs):
        total = left_ref[k].astype(F32) + right_ref[k].astype(F32)
        dens = denominators_of(total, feats)
        ref[...] = with_denominators(
            [total[:, h * HD : (h + 1) * HD] for h in range(feats // HD)],
            [dens[:, h : h + 1] for h in range(feats // HD)],
        )


def attend_kernel(part_count, skip, count, *refs):
    part_refs, refs = refs[:part_count], refs[part_count:]
    key_ref, extended_ref, valid_ref, own_ref, mask_ref, gate_hbm, up_hbm = refs[:7]
    outs = 1 if part_count == 1 else 2
    out_refs, chosen_ref, refs = refs[7 : 7 + outs], refs[7 + outs], refs[8 + outs :]
    early = early_copies(skip, count, gate_hbm, up_hbm, refs[0], refs[-1])
    for copy in early:
        copy.start()
    refs = refs[1 if count else 0 :]
    query_ref, weight_ref, total_ref, rows_ref = refs[:4]
    if part_count == 1:
        for w in range(part_refs[0].shape[0]):
            count = part_refs[0].shape[1]
            rows_ref[w * count : (w + 1) * count, :] = part_refs[0][w].astype(F32)
    else:
        chip, core = lax.axis_index("z"), lax.axis_index("core")
        for k, ref in enumerate(part_refs):
            count = ref.shape[1]
            source = (chip + part_count - k) % part_count
            for i in range(2):
                side = core if i == 0 else 1 - core
                at = pl.ds(pl.multiple_of((source * 2 + side) * count, count), count)
                rows_ref[at, :] = ref[i].astype(F32)
    slots = key_ref.shape[0]
    groups = valid_ref.shape[0]
    stacked = query_ref.shape[0]
    feats = out_refs[0].shape[-1] - LANES
    heads = feats // HD
    span = stacked // heads
    scale = 1.0 / math.sqrt(HD)

    def one_group(g, carry):
        rows = pl.ds(pl.multiple_of(g * span, span), span)
        for h in range(heads):
            query_ref[h * span : (h + 1) * span, :] = rows_ref[
                rows, h * HD : (h + 1) * HD
            ].astype(BF16)
        query = query_ref[...]
        for n in range(slots):
            scores = lax.dot_general(query, key_ref[n], NT, preferred_element_type=F32)
            weights = jnp.where(valid_ref[g, n : n + 1, :] > 0, jnp.exp(scores * scale), 0.0)
            weight_ref[:, n * BLK : (n + 1) * BLK] = weights.astype(BF16)
        sums = jnp.dot(
            weight_ref[...],
            extended_ref[...].reshape(slots * BLK, 2 * HD),
            preferred_element_type=F32,
        )
        for h in range(heads):
            total_ref[h, rows, :] = sums[h * span : (h + 1) * span, :]
        return carry

    lax.fori_loop(0, groups, one_group, 0, unroll=groups <= 2)
    chosen_ref[...] = rows_ref[:, feats + 2 * HD :]
    keys = rows_ref[:, feats : feats + HD].astype(BF16)
    values = rows_ref[:, feats + HD : feats + 2 * HD].astype(BF16)
    scores = lax.dot_general(own_ref[...], keys, NT, preferred_element_type=F32)
    weights = jnp.where(mask_ref[...] > 0, jnp.exp(scores * scale), 0.0).astype(BF16)
    extended = jnp.concatenate([values, jnp.ones_like(values)], axis=1)
    tail = jnp.dot(weights, extended, preferred_element_type=F32)
    rows = own_ref.shape[0] // heads
    mine = pl.ds(pl.multiple_of(lax.axis_index(WIDE) * rows, rows), rows)
    for h in range(heads):
        total_ref[h, mine, :] += tail[h * rows : (h + 1) * rows, :]

    if part_count == 1:

        def pack_group(g, carry):
            rows = pl.ds(pl.multiple_of(g * span, span), span)
            out_refs[0][rows, :] = with_denominators(
                [total_ref[h, rows, :HD] for h in range(heads)],
                [total_ref[h, rows, HD:] for h in range(heads)],
            )
            return carry

        lax.fori_loop(0, groups, pack_group, 0, unroll=groups <= 2)
    else:
        for k in range(part_count):
            target = (chip + k) % part_count
            for ref, side in zip(out_refs, (core, 1 - core), strict=True):
                at = pl.ds(pl.multiple_of((target * 2 + side) * rows, rows), rows)
                ref[k] = with_denominators(
                    [total_ref[h, at, :HD] for h in range(heads)],
                    [total_ref[h, at, HD:] for h in range(heads)],
                )
    for copy in early:
        copy.wait()


def normalise(side, pieces_ref, chosen_ref, gain_ref, router_ref, stack_ref, pick_ref, norm_ref, share_ref):
    kv_count, count, feats = stack_ref.shape
    pieces, rows, _ = pieces_ref.shape
    chips = pieces // kv_count

    def place(z, carry):
        to = pl.ds(pl.multiple_of(z * rows, rows), rows)
        source = pl.ds(pl.multiple_of((z * 2 + side) * rows, rows), rows)
        pick_ref[to, :] = chosen_ref[source, :]
        for k in range(kv_count):
            stack_ref[k, to, :] = pieces_ref[k * chips + z].astype(F32)
        return carry

    lax.fori_loop(0, chips, place, 0, unroll=chips <= 8)
    block = min(64, count)
    for b in range(count // block):
        at = slice(b * block, (b + 1) * block)
        squares = jnp.zeros((block, 1), F32)
        for k in range(kv_count):
            part = stack_ref[k, at, :]
            squares += jnp.sum(part * part, axis=1, keepdims=True)
        root = lax.rsqrt(squares / (kv_count * feats) + 1e-06)
        for k in range(kv_count):
            columns = slice(k * feats, (k + 1) * feats)
            part = stack_ref[k, at, :]
            norm_ref[at, columns] = (part * root * gain_ref[columns].reshape(1, feats)).astype(BF16)
        logits = lax.dot_general(norm_ref[at, :], router_ref[...], NT, preferred_element_type=F32)
        raised = jnp.where(pick_ref[at, :E] > 0, jnp.exp(logits), 0.0)
        share = raised / jnp.sum(raised, axis=1, keepdims=True)
        share = jnp.concatenate([share, jnp.zeros((block, LANES - E), F32)], axis=1)
        share_ref[:, at] = share.T


def fetch_kernel(skip, count, pieces_ref, chosen_ref, gain_ref, router_ref, gate_hbm, up_hbm, *refs):
    norm_ref, share_ref = refs[:2]
    copies = early_copies(skip, count, gate_hbm, up_hbm, refs[2], refs[-1])
    for copy in copies:
        copy.start()
    stack_ref, pick_ref = refs[-3:-1]
    normalise(
        lax.axis_index("core"),
        pieces_ref, chosen_ref, gain_ref, router_ref, stack_ref, pick_ref, norm_ref, share_ref,
    )
    for copy in copies:
        copy.wait()


def residual_kernel(part_count, *refs):
    part_refs, stream_ref = refs[:part_count], refs[part_count]
    out_ref, spread_ref = refs[-2:]
    rows, feats = out_ref.shape
    heads = feats // HD
    if part_count == 1:
        blocks = [part_refs[0][w] for w in range(part_refs[0].shape[0])]
    else:
        blocks = [ref[...] for ref in part_refs]
    total = blocks[0].astype(F32)
    for block in blocks[1:]:
        total = total + block.astype(F32)
    dens = denominators_of(total, feats)
    parts = []
    for h in range(heads):
        at = slice(h * HD, (h + 1) * HD)
        attended = total[:, at] / dens[:, h : h + 1]
        parts.append(stream_ref[:, at] + attended.astype(BF16).astype(F32))
    residual = jnp.concatenate(parts, axis=1).astype(BF16)
    out_ref[...] = residual
    for d in range(spread_ref.shape[0]):
        spread_ref[d] = residual


def expert_kernel(
    per_unit, early_count, pieces_ref, norm_own_ref, share_own_ref, chosen_ref, gain_ref, router_ref,
    gate_hbm, up_hbm, down_hbm, *refs,
):
    early_refs = refs[:early_count]
    mine_ref, theirs_ref, slot_ref, stack_ref, pick_ref, norm_ref, half_ref, share_ref = refs[
        early_count : early_count + 8
    ]
    hidden_ref, total_ref, sems = refs[early_count + 8 :]
    kv_count, both, feats = total_ref.shape
    count = both // 2
    pieces, rows, _ = pieces_ref.shape
    chips = pieces // kv_count
    units, width, _ = gate_hbm.shape
    sources = [ref.at[l] for l in range(units) for ref in (gate_hbm, up_hbm)]
    sources += [down_hbm.at[l] for l in range(units)]
    blocks = [ref.at[i] for ref in early_refs for i in range(ref.shape[0])]
    early = len(blocks)
    blocks += [slot_ref.at[i] for i in range(len(sources) - early)]
    copies = [
        pltpu.make_async_copy(sources[i], blocks[i], sems.at[i - early])
        for i in range(early, len(sources))
    ]
    for copy in copies[:AHEAD]:
        copy.start()

    def arrive(i):
        if i >= early:
            copies[i - early].wait()
            if i - early + AHEAD < len(copies):
                copies[i - early + AHEAD].start()

    normalise(
        1 - lax.axis_index("core"),
        pieces_ref, chosen_ref, gain_ref, router_ref, stack_ref, pick_ref, norm_ref, half_ref,
    )
    share_ref[:, :count] = share_own_ref[...]
    share_ref[:, count:] = half_ref[...]
    normed = jnp.concatenate([norm_own_ref[...], norm_ref[...]], axis=0)
    first_half = lax.axis_index(WIDE) * units * per_unit
    for l in range(units):
        arrive(2 * l)
        arrive(2 * l + 1)
        gate = lax.dot_general(blocks[2 * l][...], normed, NT, preferred_element_type=F32)
        up = lax.dot_general(blocks[2 * l + 1][...], normed, NT, preferred_element_type=F32)
        weight = share_ref[pl.ds((first_half + l * per_unit) // 2, 1), :]
        hidden_ref[l] = (gate / (1.0 + jnp.exp(-gate)) * up * weight).astype(BF16)
    for l in range(units):
        i = 2 * units + l
        arrive(i)
        for k in range(kv_count):
            columns = slice(k * feats, (k + 1) * feats)
            piece = lax.dot_general(
                hidden_ref[l], blocks[i][:, columns], TN, preferred_element_type=F32
            )
            total_ref[k] = piece if l == 0 else piece + total_ref[k]

    def hand_out(z, carry):
        for ref, start in ((mine_ref, 0), (theirs_ref, count)):
            at = pl.ds(pl.multiple_of(start + z * rows, rows), rows)
            for k in range(kv_count):
                ref[k * chips + z] = total_ref[k, at, :].astype(BF16)
        return carry

    lax.fori_loop(0, chips, hand_out, 0, unroll=chips <= 8)


def add_kernel(left_ref, right_ref, out_ref):
    for i in range(out_ref.shape[0]):
        out_ref[i] = (left_ref[i].astype(F32) + right_ref[i].astype(F32)).astype(BF16)


def finish_kernel(parts_ref, residual_ref, out_ref):
    total = parts_ref[0].astype(F32)
    for i in range(1, parts_ref.shape[0]):
        total = total + parts_ref[i].astype(F32)
    total = (residual_ref[...].astype(F32) + total).astype(BF16)
    step_tok, steps, _ = out_ref.shape
    for t in range(step_tok):
        out_ref[t] = total[t * steps : (t + 1) * steps]


def local(
    stream_in,
    queries,
    new_kv,
    cache_keys,
    cache_values,
    lengths,
    page_table,
    parents,
    routes,
    norm_gain,
    router,
    gate_w,
    up_w,
    down_w,
):
    kv_count = lax.axis_size("kv")
    chips = lax.axis_size("z")
    wide_count = lax.axis_size(WIDE)
    step_tok, steps, feats = stream_in.shape
    rows = step_tok * steps
    heads = feats // HD
    groups = lengths.shape[0]
    all_rows = groups * BEAMS * steps
    slots = cache_keys.shape[1]
    halves = gate_w.shape[0]
    half_width = gate_w.shape[2]
    width = kv_count * feats
    payload = feats + 2 * HD + LANES

    packed = pl.pallas_call(
        pack_kernel,
        out_shape=result((rows, payload) if chips <= 4 else (wide_count, rows, payload), BF16),
        in_specs=[VMEM] * 3,
        out_specs=VMEM,
        name="pack",
    )(queries, new_kv, routes)
    if chips <= 4:
        pair = jnp.stack([packed, lax.ppermute(packed, "core", ((0, 1), (1, 0)))])
        parts = {0: pair}
        for k in SHIFTS:
            if k < chips:
                parts[k] = lax.ppermute(pair, "z", [(i, (i + k) % chips) for i in range(chips)])
        parts = [near(parts[k]) for k in range(chips)]
    else:
        parts = [sent(packed, WIDE)]
    per_unit = 2 if halves % 2 == 0 else 1
    units = halves // per_unit
    unit_width = per_unit * half_width
    gate_rows = far(jnp.swapaxes(gate_w, 1, 2).reshape(units, unit_width, width))
    up_rows = far(jnp.swapaxes(up_w, 1, 2).reshape(units, unit_width, width))
    down_rows = far(down_w.reshape(units, unit_width, width))
    early_count = EARLY if 2 * units >= sum(EARLY) else (0,) * len(EARLY)
    skips = [sum(early_count[:i]) for i in range(len(EARLY))]
    shapes = [[pltpu.VMEM((n, unit_width, width), BF16)] if n else [] for n in early_count]
    early_sems = [pltpu.SemaphoreType.DMA((max(n, 1),)) for n in early_count]

    keys, extended, router_rows, gain, valid, own_rows, stream, mask, *early = pl.pallas_call(
        functools.partial(stage_kernel, skips[0], early_count[0]),
        out_shape=[
            result((slots, BLK, HD), BF16),
            result((slots, BLK, 2 * HD), BF16),
            result((E, width), BF16),
            result((width,), F32),
            result((groups, slots, BLK), F32),
            result((heads * rows, HD), BF16),
            result((rows, feats), F32),
            result((heads * rows, all_rows), F32),
            *shapes[0],
        ],
        in_specs=[HBM] * 11 + [ANY],
        out_specs=[VMEM] * (8 + len(shapes[0])),
        scratch_shapes=[
            pltpu.SMEM(page_table.shape, jnp.int32),
            pltpu.SMEM(lengths.shape, jnp.int32),
            pltpu.SMEM(parents.shape[::-1], jnp.int32),
            pltpu.VMEM(queries.shape, BF16),
            pltpu.VMEM(stream_in.shape, BF16),
            pltpu.SemaphoreType.DMA((9,)),
            early_sems[0],
        ],
        compiler_params=pltpu.CompilerParams(vmem_limit_bytes=16 * MIB),
        name="stage",
    )(
        far(page_table),
        far(lengths),
        far(parents.T),
        far(cache_keys[0]),
        far(cache_values[0]),
        far(router.T),
        far(norm_gain),
        gate_rows,
        up_rows,
        far(queries),
        far(stream_in),
        packed,
    )
    near_chips = chips <= 4
    if near_chips:
        sum_shapes = [result((chips, rows, feats + LANES), BF16)] * 2
    else:
        sum_shapes = [result((all_rows, feats + LANES), BF16)]
    *sums, chosen = pl.pallas_call(
        functools.partial(attend_kernel, len(parts), skips[1], early_count[1]),
        out_shape=[
            *sum_shapes,
            result((all_rows, LANES), F32),
        ],
        in_specs=[VMEM] * (len(parts) + 5) + [HBM] * 2,
        out_specs=[VMEM] * (len(sum_shapes) + 1),
        scratch_shapes=[
            pltpu.VMEM((BEAMS * steps * heads, HD), BF16),
            pltpu.VMEM((BEAMS * steps * heads, slots * BLK), BF16),
            pltpu.VMEM((heads, all_rows, 2 * HD), F32),
            pltpu.VMEM((all_rows, payload), F32),
            early_sems[1],
        ],
        compiler_params=pltpu.CompilerParams(vmem_limit_bytes=32 * MIB),
        name="attend",
    )(
        *parts, near(keys), near(extended), near(valid), near(own_rows), near(mask),
        gate_rows, up_rows,
    )

    def bring(i, after):
        if not early_count[i]:
            return []
        return [
            pl.pallas_call(
                functools.partial(bring_kernel, skips[i], early_count[i]),
                out_shape=shapes[i],
                in_specs=[ANY, HBM, HBM],
                out_specs=[VMEM],
                scratch_shapes=[early_sems[i]],
                compiler_params=pltpu.CompilerParams(vmem_limit_bytes=MIB),
                name="bring",
            )(after, gate_rows, up_rows)[0]
        ]

    if near_chips:
        kept, passed = sums
        passed = lax.ppermute(passed, "core", ((0, 1), (1, 0)))
        brought = [pinned(block) for block in bring(2, kept)]
        early = early + brought
        merged = pl.pallas_call(
            functools.partial(merge_kernel, len(brought)),
            out_shape=[result((rows, feats + LANES), BF16)] * chips,
            in_specs=[VMEM] * 2 + [ANY] * len(brought),
            out_specs=[VMEM] * chips,
            compiler_params=pltpu.CompilerParams(vmem_limit_bytes=4 * MIB),
            name="merge",
        )(near(kept), near(passed), *brought)
        arrived = [near(merged[0])]
        for k in SHIFTS:
            if k < chips:
                pairs = [(i, (i + k) % chips) for i in range(chips)]
                arrived.append(near(lax.ppermute(merged[k], "z", pairs)))
        brought = [pinned(block) for block in bring(3, merged[0])]
        early = early + brought
    else:
        brought = []
        arrived = [near(sent(sums[0].reshape(wide_count, rows, feats + LANES), WIDE))]
    residual, copies = pl.pallas_call(
        functools.partial(residual_kernel, len(arrived)),
        out_shape=[
            result((rows, feats), BF16),
            result((kv_count * chips, rows, feats), BF16),
        ],
        in_specs=[VMEM] * (len(arrived) + 1) + [ANY] * len(brought),
        out_specs=[VMEM] * 2,
        compiler_params=pltpu.CompilerParams(vmem_limit_bytes=8 * MIB),
        name="residual",
    )(*arrived, near(stream), *brought)

    own = sent(copies, ("kv", "z"))
    other = lax.ppermute(own, "core", ((0, 1), (1, 0)))
    half = all_rows // 2
    waiting = (3 * units - sum(early_count)) * unit_width * width * 2
    expert_room = waiting + 20 * all_rows * width + 4 * MIB
    norm_own, share_own, *more = pl.pallas_call(
        functools.partial(fetch_kernel, skips[4], early_count[4]),
        out_shape=[result((half, width), BF16), result((LANES, half), F32), *shapes[4]],
        in_specs=[VMEM] * 4 + [HBM] * 2,
        out_specs=[VMEM] * (2 + len(shapes[4])),
        scratch_shapes=[
            pltpu.VMEM((kv_count, half, feats), F32),
            pltpu.VMEM((half, LANES), F32),
            early_sems[4],
        ],
        compiler_params=pltpu.CompilerParams(vmem_limit_bytes=16 * MIB),
        name="fetch",
    )(near(own), near(chosen), near(gain), near(router_rows), gate_rows, up_rows)
    early = early + more
    mine, theirs = pl.pallas_call(
        functools.partial(expert_kernel, per_unit, len(early)),
        out_shape=[result((kv_count * chips, rows, feats), BF16)] * 2,
        in_specs=[VMEM] * 6 + [HBM] * 3 + [VMEM] * len(early),
        out_specs=[VMEM] * 2,
        scratch_shapes=[
            pltpu.VMEM((3 * units - sum(early_count), unit_width, width), BF16),
            pltpu.VMEM((kv_count, half, feats), F32),
            pltpu.VMEM((half, LANES), F32),
            pltpu.VMEM((half, width), BF16),
            pltpu.VMEM((LANES, half), F32),
            pltpu.VMEM((LANES, all_rows), F32),
            pltpu.VMEM((units, unit_width, all_rows), BF16),
            pltpu.VMEM((kv_count, all_rows, feats), F32),
            pltpu.SemaphoreType.DMA((3 * units,)),
        ],
        compiler_params=pltpu.CompilerParams(vmem_limit_bytes=expert_room),
        cost_estimate=pl.CostEstimate(
            flops=6 * all_rows * halves * half_width * width,
            bytes_accessed=6 * halves * half_width * width,
            transcendentals=0,
        ),
        name="experts",
    )(
        near(other),
        near(norm_own),
        near(share_own),
        near(chosen),
        near(gain),
        near(router_rows),
        gate_rows,
        up_rows,
        down_rows,
        *[pinned(block) for block in early],
    )
    swapped = lax.ppermute(theirs, "core", ((0, 1), (1, 0)))
    both = pl.pallas_call(
        add_kernel,
        out_shape=result(mine.shape, BF16),
        in_specs=[VMEM] * 2,
        out_specs=VMEM,
        name="add",
    )(near(mine), near(swapped))
    returned = sent(both, ("kv", "z"))
    return pl.pallas_call(
        finish_kernel,
        out_shape=jax.ShapeDtypeStruct(stream_in.shape, BF16),
        in_specs=[VMEM] * 2,
        out_specs=VMEM,
        name="finish",
    )(near(returned), near(residual))


def solution(mesh):
    kv_count, wide_count = mesh.devices.shape
    split = Mesh(mesh.devices.reshape(kv_count, wide_count // 2, 2), ("kv",) + WIDE)
    return jax.shard_map(
        local,
        mesh=split,
        in_specs=(
            P(WIDE, None, "kv"),
            P(WIDE, None, "kv"),
            P(WIDE, None, None, "kv"),
            P("kv", WIDE, None, None),
            P("kv", WIDE, None, None),
            P(),
            P(),
            P(),
            P(WIDE, None, None),
            P(),
            P(),
            P(WIDE, None, "kv"),
            P(WIDE, None, "kv"),
            P(WIDE, "kv", None),
        ),
        out_specs=P(WIDE, None, "kv"),
        check_vma=False,
    )
```

```python
import functools
import math

import jax
import jax.numpy as jnp
from jax import lax
from jax.experimental import pallas as pl
from jax.experimental.pallas import tpu as pltpu
from jax.sharding import Mesh
from jax.sharding import PartitionSpec as P

HD = 128
E = 64
BEAMS = 8
BLK = 128
LANES = 128
MIB = 2**20
AHEAD = 6
EARLY = (0, 0, 0, 5, 1)
SHIFTS = (3, 2, 1)
F32 = jnp.float32
BF16 = jnp.bfloat16
NT = (((1,), (1,)), ((), ()))
TN = (((0,), (0,)), ((), ()))
VMEM = pl.BlockSpec(memory_space=pltpu.VMEM)
HBM = pl.BlockSpec(memory_space=pltpu.HBM)
ANY = pl.BlockSpec(memory_space=pl.ANY)
WIDE = ("z", "core")


def small(shape, dtype):
    return math.prod(shape) * jnp.dtype(dtype).itemsize <= MIB


def near(array):
    if small(array.shape, array.dtype):
        return pltpu.with_memory_space_constraint(array, pltpu.VMEM)
    return array


def far(array):
    return pltpu.with_memory_space_constraint(array, pltpu.HBM)


def pinned(array):
    return pltpu.with_memory_space_constraint(array, pltpu.VMEM)


def result(shape, dtype):
    if small(shape, dtype):
        return pltpu.VMEM(shape, dtype)
    return jax.ShapeDtypeStruct(shape, dtype)


def sent(block, axes):
    return lax.all_to_all(block, axes, split_axis=0, concat_axis=0, tiled=True)


def pack_kernel(query_ref, new_ref, route_ref, out_ref):
    step_tok, steps, feats = query_ref.shape
    lanes = lax.broadcasted_iota(jnp.int32, (steps, LANES), 1)
    parts = []
    for t in range(step_tok):
        named = route_ref[t]
        chosen = jnp.zeros((steps, LANES), F32)
        for i in range(named.shape[1]):
            chosen = jnp.where(named[:, i : i + 1] == lanes, 1.0, chosen)
        parts.append(
            jnp.concatenate(
                [
                    query_ref[t].astype(F32),
                    new_ref[t, :, 0, :].astype(F32),
                    new_ref[t, :, 1, :].astype(F32),
                    chosen,
                ],
                axis=1,
            )
        )
    block = jnp.concatenate(parts, axis=0).astype(BF16)
    if len(out_ref.shape) == 2:
        out_ref[...] = block
    else:
        for w in range(out_ref.shape[0]):
            out_ref[w] = block


def early_copies(skip, count, gate_hbm, up_hbm, early_ref, sems):
    return [
        pltpu.make_async_copy(
            (gate_hbm, up_hbm)[(i + skip) % 2].at[(i + skip) // 2], early_ref.at[i], sems.at[i]
        )
        for i in range(count)
    ]


def stage_kernel(
    skip, count, table_hbm, length_hbm, parent_hbm, key_hbm, value_hbm, router_hbm, gain_hbm,
    gate_hbm, up_hbm, query_hbm, stream_hbm, after_ref,
    key_ref, extended_ref, router_ref, gain_ref, valid_ref, own_ref, own_stream_ref, mask_ref, *refs,
):
    del after_ref
    table_ref, length_ref, parent_ref, query_ref, stream_ref, sems = refs[-7:-1]
    early = early_copies(skip, count, gate_hbm, up_hbm, refs[0], refs[-1])
    first = [
        pltpu.make_async_copy(table_hbm, table_ref, sems.at[4]),
        pltpu.make_async_copy(length_hbm, length_ref, sems.at[5]),
        pltpu.make_async_copy(parent_hbm, parent_ref, sems.at[6]),
        pltpu.make_async_copy(query_hbm, query_ref, sems.at[7]),
        pltpu.make_async_copy(stream_hbm, stream_ref, sems.at[8]),
    ]
    for copy in first:
        copy.start()
    slots = key_ref.shape[0]
    groups, blocks = table_ref.shape
    copies = [
        pltpu.make_async_copy(key_hbm, key_ref, sems.at[0]),
        pltpu.make_async_copy(value_hbm, extended_ref.at[:, :, pl.ds(0, HD)], sems.at[1]),
        pltpu.make_async_copy(router_hbm, router_ref, sems.at[2]),
        pltpu.make_async_copy(gain_hbm, gain_ref, sems.at[3]),
    ]
    for copy in copies + early:
        copy.start()
    extended_ref[:, :, HD:] = jnp.ones((slots, BLK, HD), BF16)
    valid_ref[...] = jnp.zeros_like(valid_ref)
    for copy in first:
        copy.wait()
    first_slot = lax.axis_index(WIDE) * slots
    place = lax.broadcasted_iota(jnp.int32, (1, BLK), 1)

    def look_group(group, carry):
        length = length_ref[group]

        def look(block, limit):
            slot = table_ref[group, block] - first_slot

            @pl.when((slot >= 0) & (slot < slots))
            def _():
                valid_ref[group, pl.ds(slot, 1), :] = jnp.where(place < limit, 1.0, 0.0)

            return limit - BLK

        lax.fori_loop(0, blocks, look, length, unroll=4)
        return carry

    lax.fori_loop(0, groups, look_group, 0, unroll=groups <= 2)
    step_tok, steps, feats = query_ref.shape
    rows = step_tok * steps
    heads = feats // HD
    own = jnp.concatenate([query_ref[t].astype(F32) for t in range(step_tok)], axis=0)
    stacked = jnp.concatenate([own[:, h * HD : (h + 1) * HD] for h in range(heads)], axis=0)
    own_ref[...] = stacked.astype(BF16)
    own_stream_ref[...] = jnp.concatenate(
        [stream_ref[t].astype(F32) for t in range(step_tok)], axis=0
    )
    first_token = lax.axis_index(WIDE) * step_tok
    row = jnp.concatenate([lax.broadcasted_iota(jnp.int32, (rows, mask_ref.shape[1]), 0)] * heads, axis=0)
    column = lax.broadcasted_iota(jnp.int32, mask_ref.shape, 1)
    mask = jnp.zeros(mask_ref.shape, F32)
    for t in range(step_tok):
        token = first_token + t
        base = token // BEAMS * BEAMS
        for s in range(steps):
            ancestor = token
            for j in range(s, -1, -1):
                hit = (row == t * steps + s) & (column == ancestor * steps + j)
                mask = jnp.where(hit, 1.0, mask)
                if j > 0:
                    ancestor = base + parent_ref[j - 1, ancestor]
    mask_ref[...] = mask
    for copy in copies + early:
        copy.wait()


def with_denominators(numerators, denominators):
    lanes = lax.broadcasted_iota(jnp.int32, (numerators[0].shape[0], LANES), 1)
    heads = len(numerators)
    last = jnp.zeros(lanes.shape, F32)
    for h, denominator in enumerate(denominators):
        high = denominator.astype(BF16).astype(F32)
        last = jnp.where(lanes == h, high, last)
        last = jnp.where(lanes == heads + h, denominator - high, last)
    return jnp.concatenate(numerators + [last], axis=1).astype(BF16)


def denominators_of(total, feats):
    heads = feats // HD
    return total[:, feats : feats + heads] + total[:, feats + heads : feats + 2 * heads]


def bring_kernel(skip, count, after_ref, gate_hbm, up_hbm, early_ref, sems):
    del after_ref
    copies = early_copies(skip, count, gate_hbm, up_hbm, early_ref, sems)
    for copy in copies:
        copy.start()
    for copy in copies:
        copy.wait()


def merge_kernel(held, left_ref, right_ref, *out_refs):
    out_refs = out_refs[held:]
    feats = left_ref.shape[2] - LANES
    for k, ref in enumerate(out_refs):
        total = left_ref[k].astype(F32) + right_ref[k].astype(F32)
        dens = denominators_of(total, feats)
        ref[...] = with_denominators(
            [total[:, h * HD : (h + 1) * HD] for h in range(feats // HD)],
            [dens[:, h : h + 1] for h in range(feats // HD)],
        )


def attend_kernel(part_count, skip, count, *refs):
    part_refs, refs = refs[:part_count], refs[part_count:]
    key_ref, extended_ref, valid_ref, own_ref, mask_ref, gate_hbm, up_hbm = refs[:7]
    outs = 1 if part_count == 1 else 2
    out_refs, chosen_ref, refs = refs[7 : 7 + outs], refs[7 + outs], refs[8 + outs :]
    early = early_copies(skip, count, gate_hbm, up_hbm, refs[0], refs[-1])
    for copy in early:
        copy.start()
    refs = refs[1 if count else 0 :]
    query_ref, weight_ref, total_ref, rows_ref = refs[:4]
    if part_count == 1:
        for w in range(part_refs[0].shape[0]):
            count = part_refs[0].shape[1]
            rows_ref[w * count : (w + 1) * count, :] = part_refs[0][w].astype(F32)
    else:
        chip, core = lax.axis_index("z"), lax.axis_index("core")
        for k, ref in enumerate(part_refs):
            count = ref.shape[1]
            source = (chip + part_count - k) % part_count
            for i in range(2):
                side = core if i == 0 else 1 - core
                at = pl.ds(pl.multiple_of((source * 2 + side) * count, count), count)
                rows_ref[at, :] = ref[i].astype(F32)
    slots = key_ref.shape[0]
    groups = valid_ref.shape[0]
    stacked = query_ref.shape[0]
    feats = out_refs[0].shape[-1] - LANES
    heads = feats // HD
    span = stacked // heads
    scale = 1.0 / math.sqrt(HD)

    def one_group(g, carry):
        rows = pl.ds(pl.multiple_of(g * span, span), span)
        for h in range(heads):
            query_ref[h * span : (h + 1) * span, :] = rows_ref[
                rows, h * HD : (h + 1) * HD
            ].astype(BF16)
        query = query_ref[...]
        for n in range(slots):
            scores = lax.dot_general(query, key_ref[n], NT, preferred_element_type=F32)
            weights = jnp.where(valid_ref[g, n : n + 1, :] > 0, jnp.exp(scores * scale), 0.0)
            weight_ref[:, n * BLK : (n + 1) * BLK] = weights.astype(BF16)
        sums = jnp.dot(
            weight_ref[...],
            extended_ref[...].reshape(slots * BLK, 2 * HD),
            preferred_element_type=F32,
        )
        for h in range(heads):
            total_ref[h, rows, :] = sums[h * span : (h + 1) * span, :]
        return carry

    lax.fori_loop(0, groups, one_group, 0, unroll=groups <= 2)
    chosen_ref[...] = rows_ref[:, feats + 2 * HD :]
    keys = rows_ref[:, feats : feats + HD].astype(BF16)
    values = rows_ref[:, feats + HD : feats + 2 * HD].astype(BF16)
    scores = lax.dot_general(own_ref[...], keys, NT, preferred_element_type=F32)
    weights = jnp.where(mask_ref[...] > 0, jnp.exp(scores * scale), 0.0).astype(BF16)
    extended = jnp.concatenate([values, jnp.ones_like(values)], axis=1)
    tail = jnp.dot(weights, extended, preferred_element_type=F32)
    rows = own_ref.shape[0] // heads
    mine = pl.ds(pl.multiple_of(lax.axis_index(WIDE) * rows, rows), rows)
    for h in range(heads):
        total_ref[h, mine, :] += tail[h * rows : (h + 1) * rows, :]

    if part_count == 1:

        def pack_group(g, carry):
            rows = pl.ds(pl.multiple_of(g * span, span), span)
            out_refs[0][rows, :] = with_denominators(
                [total_ref[h, rows, :HD] for h in range(heads)],
                [total_ref[h, rows, HD:] for h in range(heads)],
            )
            return carry

        lax.fori_loop(0, groups, pack_group, 0, unroll=groups <= 2)
    else:
        for k in range(part_count):
            target = (chip + k) % part_count
            for ref, side in zip(out_refs, (core, 1 - core), strict=True):
                at = pl.ds(pl.multiple_of((target * 2 + side) * rows, rows), rows)
                ref[k] = with_denominators(
                    [total_ref[h, at, :HD] for h in range(heads)],
                    [total_ref[h, at, HD:] for h in range(heads)],
                )
    for copy in early:
        copy.wait()


def normalise(side, pieces_ref, chosen_ref, gain_ref, router_ref, stack_ref, pick_ref, norm_ref, share_ref):
    kv_count, count, feats = stack_ref.shape
    pieces, rows, _ = pieces_ref.shape
    chips = pieces // kv_count

    def place(z, carry):
        to = pl.ds(pl.multiple_of(z * rows, rows), rows)
        source = pl.ds(pl.multiple_of((z * 2 + side) * rows, rows), rows)
        pick_ref[to, :] = chosen_ref[source, :]
        for k in range(kv_count):
            stack_ref[k, to, :] = pieces_ref[k * chips + z].astype(F32)
        return carry

    lax.fori_loop(0, chips, place, 0, unroll=chips <= 8)
    block = min(64, count)
    for b in range(count // block):
        at = slice(b * block, (b + 1) * block)
        squares = jnp.zeros((block, 1), F32)
        for k in range(kv_count):
            part = stack_ref[k, at, :]
            squares += jnp.sum(part * part, axis=1, keepdims=True)
        root = lax.rsqrt(squares / (kv_count * feats) + 1e-06)
        for k in range(kv_count):
            columns = slice(k * feats, (k + 1) * feats)
            part = stack_ref[k, at, :]
            norm_ref[at, columns] = (part * root * gain_ref[columns].reshape(1, feats)).astype(BF16)
        logits = lax.dot_general(norm_ref[at, :], router_ref[...], NT, preferred_element_type=F32)
        raised = jnp.where(pick_ref[at, :E] > 0, jnp.exp(logits), 0.0)
        share = raised / jnp.sum(raised, axis=1, keepdims=True)
        share = jnp.concatenate([share, jnp.zeros((block, LANES - E), F32)], axis=1)
        share_ref[:, at] = share.T


def fetch_kernel(skip, count, pieces_ref, chosen_ref, gain_ref, router_ref, gate_hbm, up_hbm, *refs):
    norm_ref, share_ref = refs[:2]
    copies = early_copies(skip, count, gate_hbm, up_hbm, refs[2], refs[-1])
    for copy in copies:
        copy.start()
    stack_ref, pick_ref = refs[-3:-1]
    normalise(
        lax.axis_index("core"),
        pieces_ref, chosen_ref, gain_ref, router_ref, stack_ref, pick_ref, norm_ref, share_ref,
    )
    for copy in copies:
        copy.wait()


def residual_kernel(part_count, *refs):
    part_refs, stream_ref = refs[:part_count], refs[part_count]
    out_ref, spread_ref = refs[-2:]
    rows, feats = out_ref.shape
    heads = feats // HD
    if part_count == 1:
        blocks = [part_refs[0][w] for w in range(part_refs[0].shape[0])]
    else:
        blocks = [ref[...] for ref in part_refs]
    total = blocks[0].astype(F32)
    for block in blocks[1:]:
        total = total + block.astype(F32)
    dens = denominators_of(total, feats)
    parts = []
    for h in range(heads):
        at = slice(h * HD, (h + 1) * HD)
        attended = total[:, at] / dens[:, h : h + 1]
        parts.append(stream_ref[:, at] + attended.astype(BF16).astype(F32))
    residual = jnp.concatenate(parts, axis=1).astype(BF16)
    out_ref[...] = residual
    for d in range(spread_ref.shape[0]):
        spread_ref[d] = residual


def expert_kernel(
    per_unit, early_count, pieces_ref, norm_own_ref, share_own_ref, chosen_ref, gain_ref, router_ref,
    gate_hbm, up_hbm, down_hbm, *refs,
):
    early_refs = refs[:early_count]
    mine_ref, theirs_ref, slot_ref, stack_ref, pick_ref, norm_ref, half_ref, share_ref = refs[
        early_count : early_count + 8
    ]
    hidden_ref, total_ref, sems = refs[early_count + 8 :]
    kv_count, both, feats = total_ref.shape
    count = both // 2
    pieces, rows, _ = pieces_ref.shape
    chips = pieces // kv_count
    units, width, _ = gate_hbm.shape
    sources = [ref.at[l] for l in range(units) for ref in (gate_hbm, up_hbm)]
    sources += [down_hbm.at[l] for l in range(units)]
    blocks = [ref.at[i] for ref in early_refs for i in range(ref.shape[0])]
    early = len(blocks)
    blocks += [slot_ref.at[i] for i in range(len(sources) - early)]
    copies = [
        pltpu.make_async_copy(sources[i], blocks[i], sems.at[i - early])
        for i in range(early, len(sources))
    ]
    for copy in copies[:AHEAD]:
        copy.start()

    def arrive(i):
        if i >= early:
            copies[i - early].wait()
            if i - early + AHEAD < len(copies):
                copies[i - early + AHEAD].start()

    normalise(
        1 - lax.axis_index("core"),
        pieces_ref, chosen_ref, gain_ref, router_ref, stack_ref, pick_ref, norm_ref, half_ref,
    )
    share_ref[:, :count] = share_own_ref[...]
    share_ref[:, count:] = half_ref[...]
    normed = jnp.concatenate([norm_own_ref[...], norm_ref[...]], axis=0)
    first_half = lax.axis_index(WIDE) * units * per_unit
    for l in range(units):
        arrive(2 * l)
        arrive(2 * l + 1)
        gate = lax.dot_general(blocks[2 * l][...], normed, NT, preferred_element_type=F32)
        up = lax.dot_general(blocks[2 * l + 1][...], normed, NT, preferred_element_type=F32)
        weight = share_ref[pl.ds((first_half + l * per_unit) // 2, 1), :]
        hidden_ref[l] = (gate / (1.0 + jnp.exp(-gate)) * up * weight).astype(BF16)
    for l in range(units):
        i = 2 * units + l
        arrive(i)
        for k in range(kv_count):
            columns = slice(k * feats, (k + 1) * feats)
            piece = lax.dot_general(
                hidden_ref[l], blocks[i][:, columns], TN, preferred_element_type=F32
            )
            total_ref[k] = piece if l == 0 else piece + total_ref[k]

    def hand_out(z, carry):
        for ref, start in ((mine_ref, 0), (theirs_ref, count)):
            at = pl.ds(pl.multiple_of(start + z * rows, rows), rows)
            for k in range(kv_count):
                ref[k * chips + z] = total_ref[k, at, :].astype(BF16)
        return carry

    lax.fori_loop(0, chips, hand_out, 0, unroll=chips <= 8)


def add_kernel(left_ref, right_ref, out_ref):
    for i in range(out_ref.shape[0]):
        out_ref[i] = (left_ref[i].astype(F32) + right_ref[i].astype(F32)).astype(BF16)


def finish_kernel(parts_ref, residual_ref, out_ref):
    total = parts_ref[0].astype(F32)
    for i in range(1, parts_ref.shape[0]):
        total = total + parts_ref[i].astype(F32)
    total = (residual_ref[...].astype(F32) + total).astype(BF16)
    step_tok, steps, _ = out_ref.shape
    for t in range(step_tok):
        out_ref[t] = total[t * steps : (t + 1) * steps]


def local(
    stream_in,
    queries,
    new_kv,
    cache_keys,
    cache_values,
    lengths,
    page_table,
    parents,
    routes,
    norm_gain,
    router,
    gate_w,
    up_w,
    down_w,
):
    kv_count = lax.axis_size("kv")
    chips = lax.axis_size("z")
    wide_count = lax.axis_size(WIDE)
    step_tok, steps, feats = stream_in.shape
    rows = step_tok * steps
    heads = feats // HD
    groups = lengths.shape[0]
    all_rows = groups * BEAMS * steps
    slots = cache_keys.shape[1]
    halves = gate_w.shape[0]
    half_width = gate_w.shape[2]
    width = kv_count * feats
    payload = feats + 2 * HD + LANES

    packed = pl.pallas_call(
        pack_kernel,
        out_shape=result((rows, payload) if chips <= 4 else (wide_count, rows, payload), BF16),
        in_specs=[VMEM] * 3,
        out_specs=VMEM,
        name="pack",
    )(queries, new_kv, routes)
    if chips <= 4:
        pair = jnp.stack([packed, lax.ppermute(packed, "core", ((0, 1), (1, 0)))])
        parts = {0: pair}
        for k in SHIFTS:
            if k < chips:
                parts[k] = lax.ppermute(pair, "z", [(i, (i + k) % chips) for i in range(chips)])
        parts = [near(parts[k]) for k in range(chips)]
    else:
        parts = [sent(packed, WIDE)]
    per_unit = 2 if halves % 2 == 0 else 1
    units = halves // per_unit
    unit_width = per_unit * half_width
    gate_rows = far(jnp.swapaxes(gate_w, 1, 2).reshape(units, unit_width, width))
    up_rows = far(jnp.swapaxes(up_w, 1, 2).reshape(units, unit_width, width))
    down_rows = far(down_w.reshape(units, unit_width, width))
    early_count = EARLY if 2 * units >= sum(EARLY) else (0,) * len(EARLY)
    skips = [sum(early_count[:i]) for i in range(len(EARLY))]
    shapes = [[pltpu.VMEM((n, unit_width, width), BF16)] if n else [] for n in early_count]
    early_sems = [pltpu.SemaphoreType.DMA((max(n, 1),)) for n in early_count]

    keys, extended, router_rows, gain, valid, own_rows, stream, mask, *early = pl.pallas_call(
        functools.partial(stage_kernel, skips[0], early_count[0]),
        out_shape=[
            result((slots, BLK, HD), BF16),
            result((slots, BLK, 2 * HD), BF16),
            result((E, width), BF16),
            result((width,), F32),
            result((groups, slots, BLK), F32),
            result((heads * rows, HD), BF16),
            result((rows, feats), F32),
            result((heads * rows, all_rows), F32),
            *shapes[0],
        ],
        in_specs=[HBM] * 11 + [ANY],
        out_specs=[VMEM] * (8 + len(shapes[0])),
        scratch_shapes=[
            pltpu.SMEM(page_table.shape, jnp.int32),
            pltpu.SMEM(lengths.shape, jnp.int32),
            pltpu.SMEM(parents.shape[::-1], jnp.int32),
            pltpu.VMEM(queries.shape, BF16),
            pltpu.VMEM(stream_in.shape, BF16),
            pltpu.SemaphoreType.DMA((9,)),
            early_sems[0],
        ],
        compiler_params=pltpu.CompilerParams(vmem_limit_bytes=16 * MIB),
        name="stage",
    )(
        far(page_table),
        far(lengths),
        far(parents.T),
        far(cache_keys[0]),
        far(cache_values[0]),
        far(router.T),
        far(norm_gain),
        gate_rows,
        up_rows,
        far(queries),
        far(stream_in),
        packed,
    )
    near_chips = chips <= 4
    if near_chips:
        sum_shapes = [result((chips, rows, feats + LANES), BF16)] * 2
    else:
        sum_shapes = [result((all_rows, feats + LANES), BF16)]
    *sums, chosen = pl.pallas_call(
        functools.partial(attend_kernel, len(parts), skips[1], early_count[1]),
        out_shape=[
            *sum_shapes,
            result((all_rows, LANES), F32),
        ],
        in_specs=[VMEM] * (len(parts) + 5) + [HBM] * 2,
        out_specs=[VMEM] * (len(sum_shapes) + 1),
        scratch_shapes=[
            pltpu.VMEM((BEAMS * steps * heads, HD), BF16),
            pltpu.VMEM((BEAMS * steps * heads, slots * BLK), BF16),
            pltpu.VMEM((heads, all_rows, 2 * HD), F32),
            pltpu.VMEM((all_rows, payload), F32),
            early_sems[1],
        ],
        compiler_params=pltpu.CompilerParams(vmem_limit_bytes=32 * MIB),
        name="attend",
    )(
        *parts, near(keys), near(extended), near(valid), near(own_rows), near(mask),
        gate_rows, up_rows,
    )

    def bring(i, after):
        if not early_count[i]:
            return []
        return [
            pl.pallas_call(
                functools.partial(bring_kernel, skips[i], early_count[i]),
                out_shape=shapes[i],
                in_specs=[ANY, HBM, HBM],
                out_specs=[VMEM],
                scratch_shapes=[early_sems[i]],
                compiler_params=pltpu.CompilerParams(vmem_limit_bytes=MIB),
                name="bring",
            )(after, gate_rows, up_rows)[0]
        ]

    if near_chips:
        kept, passed = sums
        passed = lax.ppermute(passed, "core", ((0, 1), (1, 0)))
        brought = [pinned(block) for block in bring(2, kept)]
        early = early + brought
        merged = pl.pallas_call(
            functools.partial(merge_kernel, len(brought)),
            out_shape=[result((rows, feats + LANES), BF16)] * chips,
            in_specs=[VMEM] * 2 + [ANY] * len(brought),
            out_specs=[VMEM] * chips,
            compiler_params=pltpu.CompilerParams(vmem_limit_bytes=4 * MIB),
            name="merge",
        )(near(kept), near(passed), *brought)
        arrived = [near(merged[0])]
        for k in SHIFTS:
            if k < chips:
                pairs = [(i, (i + k) % chips) for i in range(chips)]
                arrived.append(near(lax.ppermute(merged[k], "z", pairs)))
        brought = [pinned(block) for block in bring(3, merged[0])]
        early = early + brought
    else:
        brought = []
        arrived = [near(sent(sums[0].reshape(wide_count, rows, feats + LANES), WIDE))]
    residual, copies = pl.pallas_call(
        functools.partial(residual_kernel, len(arrived)),
        out_shape=[
            result((rows, feats), BF16),
            result((kv_count * chips, rows, feats), BF16),
        ],
        in_specs=[VMEM] * (len(arrived) + 1) + [ANY] * len(brought),
        out_specs=[VMEM] * 2,
        compiler_params=pltpu.CompilerParams(vmem_limit_bytes=8 * MIB),
        name="residual",
    )(*arrived, near(stream), *brought)

    own = sent(copies, ("kv", "z"))
    other = lax.ppermute(own, "core", ((0, 1), (1, 0)))
    half = all_rows // 2
    waiting = (3 * units - sum(early_count)) * unit_width * width * 2
    expert_room = waiting + 20 * all_rows * width + 4 * MIB
    norm_own, share_own, *more = pl.pallas_call(
        functools.partial(fetch_kernel, skips[4], early_count[4]),
        out_shape=[result((half, width), BF16), result((LANES, half), F32), *shapes[4]],
        in_specs=[VMEM] * 4 + [HBM] * 2,
        out_specs=[VMEM] * (2 + len(shapes[4])),
        scratch_shapes=[
            pltpu.VMEM((kv_count, half, feats), F32),
            pltpu.VMEM((half, LANES), F32),
            early_sems[4],
        ],
        compiler_params=pltpu.CompilerParams(vmem_limit_bytes=16 * MIB),
        name="fetch",
    )(near(own), near(chosen), near(gain), near(router_rows), gate_rows, up_rows)
    early = early + more
    mine, theirs = pl.pallas_call(
        functools.partial(expert_kernel, per_unit, len(early)),
        out_shape=[result((kv_count * chips, rows, feats), BF16)] * 2,
        in_specs=[VMEM] * 6 + [HBM] * 3 + [VMEM] * len(early),
        out_specs=[VMEM] * 2,
        scratch_shapes=[
            pltpu.VMEM((3 * units - sum(early_count), unit_width, width), BF16),
            pltpu.VMEM((kv_count, half, feats), F32),
            pltpu.VMEM((half, LANES), F32),
            pltpu.VMEM((half, width), BF16),
            pltpu.VMEM((LANES, half), F32),
            pltpu.VMEM((LANES, all_rows), F32),
            pltpu.VMEM((units, unit_width, all_rows), BF16),
            pltpu.VMEM((kv_count, all_rows, feats), F32),
            pltpu.SemaphoreType.DMA((3 * units,)),
        ],
        compiler_params=pltpu.CompilerParams(vmem_limit_bytes=expert_room),
        cost_estimate=pl.CostEstimate(
            flops=6 * all_rows * halves * half_width * width,
            bytes_accessed=6 * halves * half_width * width,
            transcendentals=0,
        ),
        name="experts",
    )(
        near(other),
        near(norm_own),
        near(share_own),
        near(chosen),
        near(gain),
        near(router_rows),
        gate_rows,
        up_rows,
        down_rows,
        *[pinned(block) for block in early],
    )
    swapped = lax.ppermute(theirs, "core", ((0, 1), (1, 0)))
    both = pl.pallas_call(
        add_kernel,
        out_shape=result(mine.shape, BF16),
        in_specs=[VMEM] * 2,
        out_specs=VMEM,
        name="add",
    )(near(mine), near(swapped))
    returned = sent(both, ("kv", "z"))
    return pl.pallas_call(
        finish_kernel,
        out_shape=jax.ShapeDtypeStruct(stream_in.shape, BF16),
        in_specs=[VMEM] * 2,
        out_specs=VMEM,
        name="finish",
    )(near(returned), near(residual))


def solution(mesh):
    kv_count, wide_count = mesh.devices.shape
    split = Mesh(mesh.devices.reshape(kv_count, wide_count // 2, 2), ("kv",) + WIDE)
    return jax.shard_map(
        local,
        mesh=split,
        in_specs=(
            P(WIDE, None, "kv"),
            P(WIDE, None, "kv"),
            P(WIDE, None, None, "kv"),
            P("kv", WIDE, None, None),
            P("kv", WIDE, None, None),
            P(),
            P(),
            P(),
            P(WIDE, None, None),
            P(),
            P(),
            P(WIDE, None, "kv"),
            P(WIDE, None, "kv"),
            P(WIDE, "kv", None),
        ),
        out_specs=P(WIDE, None, "kv"),
        check_vma=False,
    )
```

```python
import functools
import math

import jax
import jax.numpy as jnp
from jax import lax
from jax.experimental import pallas as pl
from jax.experimental.pallas import tpu as pltpu
from jax.sharding import Mesh
from jax.sharding import PartitionSpec as P

HD = 128
E = 64
BEAMS = 8
BLK = 128
LANES = 128
MIB = 2**20
AHEAD = 6
EARLY = (0, 0, 0, 5, 1)
SHIFTS = (3, 2, 1)
F32 = jnp.float32
BF16 = jnp.bfloat16
NT = (((1,), (1,)), ((), ()))
TN = (((0,), (0,)), ((), ()))
VMEM = pl.BlockSpec(memory_space=pltpu.VMEM)
HBM = pl.BlockSpec(memory_space=pltpu.HBM)
ANY = pl.BlockSpec(memory_space=pl.ANY)
WIDE = ("z", "core")


def small(shape, dtype):
    return math.prod(shape) * jnp.dtype(dtype).itemsize <= MIB


def near(array):
    if small(array.shape, array.dtype):
        return pltpu.with_memory_space_constraint(array, pltpu.VMEM)
    return array


def far(array):
    return pltpu.with_memory_space_constraint(array, pltpu.HBM)


def pinned(array):
    return pltpu.with_memory_space_constraint(array, pltpu.VMEM)


def result(shape, dtype):
    if small(shape, dtype):
        return pltpu.VMEM(shape, dtype)
    return jax.ShapeDtypeStruct(shape, dtype)


def sent(block, axes):
    return lax.all_to_all(block, axes, split_axis=0, concat_axis=0, tiled=True)


def pack_kernel(query_ref, new_ref, route_ref, out_ref):
    step_tok, steps, feats = query_ref.shape
    lanes = lax.broadcasted_iota(jnp.int32, (steps, LANES), 1)
    parts = []
    for t in range(step_tok):
        named = route_ref[t]
        chosen = jnp.zeros((steps, LANES), F32)
        for i in range(named.shape[1]):
            chosen = jnp.where(named[:, i : i + 1] == lanes, 1.0, chosen)
        parts.append(
            jnp.concatenate(
                [
                    query_ref[t].astype(F32),
                    new_ref[t, :, 0, :].astype(F32),
                    new_ref[t, :, 1, :].astype(F32),
                    chosen,
                ],
                axis=1,
            )
        )
    block = jnp.concatenate(parts, axis=0).astype(BF16)
    if len(out_ref.shape) == 2:
        out_ref[...] = block
    else:
        for w in range(out_ref.shape[0]):
            out_ref[w] = block


def early_copies(skip, count, gate_hbm, up_hbm, early_ref, sems):
    return [
        pltpu.make_async_copy(
            (gate_hbm, up_hbm)[(i + skip) % 2].at[(i + skip) // 2], early_ref.at[i], sems.at[i]
        )
        for i in range(count)
    ]


def stage_kernel(
    skip, count, table_hbm, length_hbm, parent_hbm, key_hbm, value_hbm, router_hbm, gain_hbm,
    gate_hbm, up_hbm, query_ref, stream_ref, after_ref,
    key_ref, extended_ref, router_ref, gain_ref, valid_ref, own_ref, own_stream_ref, mask_ref, *refs,
):
    del after_ref
    table_ref, length_ref, parent_ref, sems = refs[-5:-1]
    early = early_copies(skip, count, gate_hbm, up_hbm, refs[0], refs[-1])
    first = [
        pltpu.make_async_copy(table_hbm, table_ref, sems.at[4]),
        pltpu.make_async_copy(length_hbm, length_ref, sems.at[5]),
        pltpu.make_async_copy(parent_hbm, parent_ref, sems.at[6]),
    ]
    for copy in first:
        copy.start()
    slots = key_ref.shape[0]
    groups, blocks = table_ref.shape
    copies = [
        pltpu.make_async_copy(key_hbm, key_ref, sems.at[0]),
        pltpu.make_async_copy(value_hbm, extended_ref.at[:, :, pl.ds(0, HD)], sems.at[1]),
        pltpu.make_async_copy(router_hbm, router_ref, sems.at[2]),
        pltpu.make_async_copy(gain_hbm, gain_ref, sems.at[3]),
    ]
    for copy in copies + early:
        copy.start()
    extended_ref[:, :, HD:] = jnp.ones((slots, BLK, HD), BF16)
    valid_ref[...] = jnp.zeros_like(valid_ref)
    for copy in first:
        copy.wait()
    first_slot = lax.axis_index(WIDE) * slots
    place = lax.broadcasted_iota(jnp.int32, (1, BLK), 1)

    def look_group(group, carry):
        length = length_ref[group]

        def look(block, limit):
            slot = table_ref[group, block] - first_slot

            @pl.when((slot >= 0) & (slot < slots))
            def _():
                valid_ref[group, pl.ds(slot, 1), :] = jnp.where(place < limit, 1.0, 0.0)

            return limit - BLK

        lax.fori_loop(0, blocks, look, length, unroll=4)
        return carry

    lax.fori_loop(0, groups, look_group, 0, unroll=groups <= 2)
    step_tok, steps, feats = query_ref.shape
    rows = step_tok * steps
    heads = feats // HD
    own = jnp.concatenate([query_ref[t].astype(F32) for t in range(step_tok)], axis=0)
    stacked = jnp.concatenate([own[:, h * HD : (h + 1) * HD] for h in range(heads)], axis=0)
    own_ref[...] = stacked.astype(BF16)
    own_stream_ref[...] = jnp.concatenate(
        [stream_ref[t].astype(F32) for t in range(step_tok)], axis=0
    )
    first_token = lax.axis_index(WIDE) * step_tok
    row = jnp.concatenate([lax.broadcasted_iota(jnp.int32, (rows, mask_ref.shape[1]), 0)] * heads, axis=0)
    column = lax.broadcasted_iota(jnp.int32, mask_ref.shape, 1)
    mask = jnp.zeros(mask_ref.shape, F32)
    for t in range(step_tok):
        token = first_token + t
        base = token // BEAMS * BEAMS
        for s in range(steps):
            ancestor = token
            for j in range(s, -1, -1):
                hit = (row == t * steps + s) & (column == ancestor * steps + j)
                mask = jnp.where(hit, 1.0, mask)
                if j > 0:
                    ancestor = base + parent_ref[j - 1, ancestor]
    mask_ref[...] = mask
    for copy in copies + early:
        copy.wait()


def with_denominators(numerators, denominators):
    lanes = lax.broadcasted_iota(jnp.int32, (numerators[0].shape[0], LANES), 1)
    heads = len(numerators)
    last = jnp.zeros(lanes.shape, F32)
    for h, denominator in enumerate(denominators):
        high = denominator.astype(BF16).astype(F32)
        last = jnp.where(lanes == h, high, last)
        last = jnp.where(lanes == heads + h, denominator - high, last)
    return jnp.concatenate(numerators + [last], axis=1).astype(BF16)


def denominators_of(total, feats):
    heads = feats // HD
    return total[:, feats : feats + heads] + total[:, feats + heads : feats + 2 * heads]


def bring_kernel(skip, count, after_ref, gate_hbm, up_hbm, early_ref, sems):
    del after_ref
    copies = early_copies(skip, count, gate_hbm, up_hbm, early_ref, sems)
    for copy in copies:
        copy.start()
    for copy in copies:
        copy.wait()


def merge_kernel(held, left_ref, right_ref, *out_refs):
    out_refs = out_refs[held:]
    feats = left_ref.shape[2] - LANES
    for k, ref in enumerate(out_refs):
        total = left_ref[k].astype(F32) + right_ref[k].astype(F32)
        dens = denominators_of(total, feats)
        ref[...] = with_denominators(
            [total[:, h * HD : (h + 1) * HD] for h in range(feats // HD)],
            [dens[:, h : h + 1] for h in range(feats // HD)],
        )


def attend_kernel(part_count, skip, count, *refs):
    part_refs, refs = refs[:part_count], refs[part_count:]
    key_ref, extended_ref, valid_ref, own_ref, mask_ref, gate_hbm, up_hbm = refs[:7]
    outs = 1 if part_count == 1 else 2
    out_refs, chosen_ref, refs = refs[7 : 7 + outs], refs[7 + outs], refs[8 + outs :]
    early = early_copies(skip, count, gate_hbm, up_hbm, refs[0], refs[-1])
    for copy in early:
        copy.start()
    refs = refs[1 if count else 0 :]
    query_ref, weight_ref, total_ref, rows_ref = refs[:4]
    if part_count == 1:
        for w in range(part_refs[0].shape[0]):
            count = part_refs[0].shape[1]
            rows_ref[w * count : (w + 1) * count, :] = part_refs[0][w].astype(F32)
    else:
        chip, core = lax.axis_index("z"), lax.axis_index("core")
        for k, ref in enumerate(part_refs):
            count = ref.shape[1]
            source = (chip + part_count - k) % part_count
            for i in range(2):
                side = core if i == 0 else 1 - core
                at = pl.ds(pl.multiple_of((source * 2 + side) * count, count), count)
                rows_ref[at, :] = ref[i].astype(F32)
    slots = key_ref.shape[0]
    groups = valid_ref.shape[0]
    stacked = query_ref.shape[0]
    feats = out_refs[0].shape[-1] - LANES
    heads = feats // HD
    span = stacked // heads
    scale = 1.0 / math.sqrt(HD)

    def one_group(g, carry):
        rows = pl.ds(pl.multiple_of(g * span, span), span)
        for h in range(heads):
            query_ref[h * span : (h + 1) * span, :] = rows_ref[
                rows, h * HD : (h + 1) * HD
            ].astype(BF16)
        query = query_ref[...]
        for n in range(slots):
            scores = lax.dot_general(query, key_ref[n], NT, preferred_element_type=F32)
            weights = jnp.where(valid_ref[g, n : n + 1, :] > 0, jnp.exp(scores * scale), 0.0)
            weight_ref[:, n * BLK : (n + 1) * BLK] = weights.astype(BF16)
        sums = jnp.dot(
            weight_ref[...],
            extended_ref[...].reshape(slots * BLK, 2 * HD),
            preferred_element_type=F32,
        )
        for h in range(heads):
            total_ref[h, rows, :] = sums[h * span : (h + 1) * span, :]
        return carry

    lax.fori_loop(0, groups, one_group, 0, unroll=groups <= 2)
    chosen_ref[...] = rows_ref[:, feats + 2 * HD :]
    keys = rows_ref[:, feats : feats + HD].astype(BF16)
    values = rows_ref[:, feats + HD : feats + 2 * HD].astype(BF16)
    scores = lax.dot_general(own_ref[...], keys, NT, preferred_element_type=F32)
    weights = jnp.where(mask_ref[...] > 0, jnp.exp(scores * scale), 0.0).astype(BF16)
    extended = jnp.concatenate([values, jnp.ones_like(values)], axis=1)
    tail = jnp.dot(weights, extended, preferred_element_type=F32)
    rows = own_ref.shape[0] // heads
    mine = pl.ds(pl.multiple_of(lax.axis_index(WIDE) * rows, rows), rows)
    for h in range(heads):
        total_ref[h, mine, :] += tail[h * rows : (h + 1) * rows, :]

    if part_count == 1:

        def pack_group(g, carry):
            rows = pl.ds(pl.multiple_of(g * span, span), span)
            out_refs[0][rows, :] = with_denominators(
                [total_ref[h, rows, :HD] for h in range(heads)],
                [total_ref[h, rows, HD:] for h in range(heads)],
            )
            return carry

        lax.fori_loop(0, groups, pack_group, 0, unroll=groups <= 2)
    else:
        for k in range(part_count):
            target = (chip + k) % part_count
            for ref, side in zip(out_refs, (core, 1 - core), strict=True):
                at = pl.ds(pl.multiple_of((target * 2 + side) * rows, rows), rows)
                ref[k] = with_denominators(
                    [total_ref[h, at, :HD] for h in range(heads)],
                    [total_ref[h, at, HD:] for h in range(heads)],
                )
    for copy in early:
        copy.wait()


def normalise(side, pieces_ref, chosen_ref, gain_ref, router_ref, stack_ref, pick_ref, norm_ref, share_ref):
    kv_count, count, feats = stack_ref.shape
    pieces, rows, _ = pieces_ref.shape
    chips = pieces // kv_count

    def place(z, carry):
        to = pl.ds(pl.multiple_of(z * rows, rows), rows)
        source = pl.ds(pl.multiple_of((z * 2 + side) * rows, rows), rows)
        pick_ref[to, :] = chosen_ref[source, :]
        for k in range(kv_count):
            stack_ref[k, to, :] = pieces_ref[k * chips + z].astype(F32)
        return carry

    lax.fori_loop(0, chips, place, 0, unroll=chips <= 8)
    block = min(64, count)
    for b in range(count // block):
        at = slice(b * block, (b + 1) * block)
        squares = jnp.zeros((block, 1), F32)
        for k in range(kv_count):
            part = stack_ref[k, at, :]
            squares += jnp.sum(part * part, axis=1, keepdims=True)
        root = lax.rsqrt(squares / (kv_count * feats) + 1e-06)
        for k in range(kv_count):
            columns = slice(k * feats, (k + 1) * feats)
            part = stack_ref[k, at, :]
            norm_ref[at, columns] = (part * root * gain_ref[columns].reshape(1, feats)).astype(BF16)
        logits = lax.dot_general(norm_ref[at, :], router_ref[...], NT, preferred_element_type=F32)
        raised = jnp.where(pick_ref[at, :E] > 0, jnp.exp(logits), 0.0)
        share = raised / jnp.sum(raised, axis=1, keepdims=True)
        share = jnp.concatenate([share, jnp.zeros((block, LANES - E), F32)], axis=1)
        share_ref[:, at] = share.T


def fetch_kernel(skip, count, pieces_ref, chosen_ref, gain_ref, router_ref, gate_hbm, up_hbm, *refs):
    norm_ref, share_ref = refs[:2]
    copies = early_copies(skip, count, gate_hbm, up_hbm, refs[2], refs[-1])
    for copy in copies:
        copy.start()
    stack_ref, pick_ref = refs[-3:-1]
    normalise(
        lax.axis_index("core"),
        pieces_ref, chosen_ref, gain_ref, router_ref, stack_ref, pick_ref, norm_ref, share_ref,
    )
    for copy in copies:
        copy.wait()


def residual_kernel(part_count, *refs):
    part_refs, stream_ref = refs[:part_count], refs[part_count]
    out_ref, spread_ref = refs[-2:]
    rows, feats = out_ref.shape
    heads = feats // HD
    if part_count == 1:
        blocks = [part_refs[0][w] for w in range(part_refs[0].shape[0])]
    else:
        blocks = [ref[...] for ref in part_refs]
    total = blocks[0].astype(F32)
    for block in blocks[1:]:
        total = total + block.astype(F32)
    dens = denominators_of(total, feats)
    parts = []
    for h in range(heads):
        at = slice(h * HD, (h + 1) * HD)
        attended = total[:, at] / dens[:, h : h + 1]
        parts.append(stream_ref[:, at] + attended.astype(BF16).astype(F32))
    residual = jnp.concatenate(parts, axis=1).astype(BF16)
    out_ref[...] = residual
    for d in range(spread_ref.shape[0]):
        spread_ref[d] = residual


def expert_kernel(
    per_unit, early_count, pieces_ref, norm_own_ref, share_own_ref, chosen_ref, gain_ref, router_ref,
    gate_hbm, up_hbm, down_hbm, *refs,
):
    early_refs = refs[:early_count]
    mine_ref, theirs_ref, slot_ref, stack_ref, pick_ref, norm_ref, half_ref, share_ref = refs[
        early_count : early_count + 8
    ]
    hidden_ref, total_ref, sems = refs[early_count + 8 :]
    kv_count, both, feats = total_ref.shape
    count = both // 2
    pieces, rows, _ = pieces_ref.shape
    chips = pieces // kv_count
    units, width, _ = gate_hbm.shape
    sources = [ref.at[l] for l in range(units) for ref in (gate_hbm, up_hbm)]
    sources += [down_hbm.at[l] for l in range(units)]
    blocks = [ref.at[i] for ref in early_refs for i in range(ref.shape[0])]
    early = len(blocks)
    blocks += [slot_ref.at[i] for i in range(len(sources) - early)]
    copies = [
        pltpu.make_async_copy(sources[i], blocks[i], sems.at[i - early])
        for i in range(early, len(sources))
    ]
    for copy in copies[:AHEAD]:
        copy.start()

    def arrive(i):
        if i >= early:
            copies[i - early].wait()
            if i - early + AHEAD < len(copies):
                copies[i - early + AHEAD].start()

    normalise(
        1 - lax.axis_index("core"),
        pieces_ref, chosen_ref, gain_ref, router_ref, stack_ref, pick_ref, norm_ref, half_ref,
    )
    share_ref[:, :count] = share_own_ref[...]
    share_ref[:, count:] = half_ref[...]
    normed = jnp.concatenate([norm_own_ref[...], norm_ref[...]], axis=0)
    first_half = lax.axis_index(WIDE) * units * per_unit
    for l in range(units):
        arrive(2 * l)
        arrive(2 * l + 1)
        gate = lax.dot_general(blocks[2 * l][...], normed, NT, preferred_element_type=F32)
        up = lax.dot_general(blocks[2 * l + 1][...], normed, NT, preferred_element_type=F32)
        weight = share_ref[pl.ds((first_half + l * per_unit) // 2, 1), :]
        hidden_ref[l] = (gate / (1.0 + jnp.exp(-gate)) * up * weight).astype(BF16)
    for l in range(units):
        i = 2 * units + l
        arrive(i)
        for k in range(kv_count):
            columns = slice(k * feats, (k + 1) * feats)
            piece = lax.dot_general(
                hidden_ref[l], blocks[i][:, columns], TN, preferred_element_type=F32
            )
            total_ref[k] = piece if l == 0 else piece + total_ref[k]

    def hand_out(z, carry):
        for ref, start in ((mine_ref, 0), (theirs_ref, count)):
            at = pl.ds(pl.multiple_of(start + z * rows, rows), rows)
            for k in range(kv_count):
                ref[k * chips + z] = total_ref[k, at, :].astype(BF16)
        return carry

    lax.fori_loop(0, chips, hand_out, 0, unroll=chips <= 8)


def add_kernel(left_ref, right_ref, out_ref):
    for i in range(out_ref.shape[0]):
        out_ref[i] = (left_ref[i].astype(F32) + right_ref[i].astype(F32)).astype(BF16)


def finish_kernel(parts_ref, residual_ref, out_ref):
    total = parts_ref[0].astype(F32)
    for i in range(1, parts_ref.shape[0]):
        total = total + parts_ref[i].astype(F32)
    total = (residual_ref[...].astype(F32) + total).astype(BF16)
    step_tok, steps, _ = out_ref.shape
    for t in range(step_tok):
        out_ref[t] = total[t * steps : (t + 1) * steps]


def local(
    stream_in,
    queries,
    new_kv,
    cache_keys,
    cache_values,
    lengths,
    page_table,
    parents,
    routes,
    norm_gain,
    router,
    gate_w,
    up_w,
    down_w,
):
    kv_count = lax.axis_size("kv")
    chips = lax.axis_size("z")
    wide_count = lax.axis_size(WIDE)
    step_tok, steps, feats = stream_in.shape
    rows = step_tok * steps
    heads = feats // HD
    groups = lengths.shape[0]
    all_rows = groups * BEAMS * steps
    slots = cache_keys.shape[1]
    halves = gate_w.shape[0]
    half_width = gate_w.shape[2]
    width = kv_count * feats
    payload = feats + 2 * HD + LANES

    packed = pl.pallas_call(
        pack_kernel,
        out_shape=result((rows, payload) if chips <= 4 else (wide_count, rows, payload), BF16),
        in_specs=[VMEM] * 3,
        out_specs=VMEM,
        name="pack",
    )(queries, new_kv, routes)
    if chips <= 4:
        pair = jnp.stack([packed, lax.ppermute(packed, "core", ((0, 1), (1, 0)))])
        parts = {0: pair}
        for k in SHIFTS:
            if k < chips:
                parts[k] = lax.ppermute(pair, "z", [(i, (i + k) % chips) for i in range(chips)])
        parts = [near(parts[k]) for k in range(chips)]
    else:
        parts = [sent(packed, WIDE)]
    per_unit = 2 if halves % 2 == 0 else 1
    units = halves // per_unit
    unit_width = per_unit * half_width
    gate_rows = far(jnp.swapaxes(gate_w, 1, 2).reshape(units, unit_width, width))
    up_rows = far(jnp.swapaxes(up_w, 1, 2).reshape(units, unit_width, width))
    down_rows = far(down_w.reshape(units, unit_width, width))
    early_count = EARLY if 2 * units >= sum(EARLY) else (0,) * len(EARLY)
    skips = [sum(early_count[:i]) for i in range(len(EARLY))]
    shapes = [[pltpu.VMEM((n, unit_width, width), BF16)] if n else [] for n in early_count]
    early_sems = [pltpu.SemaphoreType.DMA((max(n, 1),)) for n in early_count]

    keys, extended, router_rows, gain, valid, own_rows, stream, mask, *early = pl.pallas_call(
        functools.partial(stage_kernel, skips[0], early_count[0]),
        out_shape=[
            result((slots, BLK, HD), BF16),
            result((slots, BLK, 2 * HD), BF16),
            result((E, width), BF16),
            result((width,), F32),
            result((groups, slots, BLK), F32),
            result((heads * rows, HD), BF16),
            result((rows, feats), F32),
            result((heads * rows, all_rows), F32),
            *shapes[0],
        ],
        in_specs=[HBM] * 9 + [VMEM] * 2 + [ANY],
        out_specs=[VMEM] * (8 + len(shapes[0])),
        scratch_shapes=[
            pltpu.SMEM(page_table.shape, jnp.int32),
            pltpu.SMEM(lengths.shape, jnp.int32),
            pltpu.SMEM(parents.shape[::-1], jnp.int32),
            pltpu.SemaphoreType.DMA((7,)),
            early_sems[0],
        ],
        compiler_params=pltpu.CompilerParams(vmem_limit_bytes=16 * MIB),
        name="stage",
    )(
        far(page_table),
        far(lengths),
        far(parents.T),
        far(cache_keys[0]),
        far(cache_values[0]),
        far(router.T),
        far(norm_gain),
        gate_rows,
        up_rows,
        far(queries),
        far(stream_in),
        packed,
    )
    near_chips = chips <= 4
    if near_chips:
        sum_shapes = [result((chips, rows, feats + LANES), BF16)] * 2
    else:
        sum_shapes = [result((all_rows, feats + LANES), BF16)]
    *sums, chosen = pl.pallas_call(
        functools.partial(attend_kernel, len(parts), skips[1], early_count[1]),
        out_shape=[
            *sum_shapes,
            result((all_rows, LANES), F32),
        ],
        in_specs=[VMEM] * (len(parts) + 5) + [HBM] * 2,
        out_specs=[VMEM] * (len(sum_shapes) + 1),
        scratch_shapes=[
            pltpu.VMEM((BEAMS * steps * heads, HD), BF16),
            pltpu.VMEM((BEAMS * steps * heads, slots * BLK), BF16),
            pltpu.VMEM((heads, all_rows, 2 * HD), F32),
            pltpu.VMEM((all_rows, payload), F32),
            early_sems[1],
        ],
        compiler_params=pltpu.CompilerParams(vmem_limit_bytes=32 * MIB),
        name="attend",
    )(
        *parts, near(keys), near(extended), near(valid), near(own_rows), near(mask),
        gate_rows, up_rows,
    )

    def bring(i, after):
        if not early_count[i]:
            return []
        return [
            pl.pallas_call(
                functools.partial(bring_kernel, skips[i], early_count[i]),
                out_shape=shapes[i],
                in_specs=[ANY, HBM, HBM],
                out_specs=[VMEM],
                scratch_shapes=[early_sems[i]],
                compiler_params=pltpu.CompilerParams(vmem_limit_bytes=MIB),
                name="bring",
            )(after, gate_rows, up_rows)[0]
        ]

    if near_chips:
        kept, passed = sums
        passed = lax.ppermute(passed, "core", ((0, 1), (1, 0)))
        brought = [pinned(block) for block in bring(2, kept)]
        early = early + brought
        merged = pl.pallas_call(
            functools.partial(merge_kernel, len(brought)),
            out_shape=[result((rows, feats + LANES), BF16)] * chips,
            in_specs=[VMEM] * 2 + [ANY] * len(brought),
            out_specs=[VMEM] * chips,
            compiler_params=pltpu.CompilerParams(vmem_limit_bytes=4 * MIB),
            name="merge",
        )(near(kept), near(passed), *brought)
        arrived = [near(merged[0])]
        for k in SHIFTS:
            if k < chips:
                pairs = [(i, (i + k) % chips) for i in range(chips)]
                arrived.append(near(lax.ppermute(merged[k], "z", pairs)))
        brought = [pinned(block) for block in bring(3, merged[0])]
        early = early + brought
    else:
        brought = []
        arrived = [near(sent(sums[0].reshape(wide_count, rows, feats + LANES), WIDE))]
    residual, copies = pl.pallas_call(
        functools.partial(residual_kernel, len(arrived)),
        out_shape=[
            result((rows, feats), BF16),
            result((kv_count * chips, rows, feats), BF16),
        ],
        in_specs=[VMEM] * (len(arrived) + 1) + [ANY] * len(brought),
        out_specs=[VMEM] * 2,
        compiler_params=pltpu.CompilerParams(vmem_limit_bytes=8 * MIB),
        name="residual",
    )(*arrived, near(stream), *brought)

    own = sent(copies, ("kv", "z"))
    other = lax.ppermute(own, "core", ((0, 1), (1, 0)))
    half = all_rows // 2
    waiting = (3 * units - sum(early_count)) * unit_width * width * 2
    expert_room = waiting + 20 * all_rows * width + 4 * MIB
    norm_own, share_own, *more = pl.pallas_call(
        functools.partial(fetch_kernel, skips[4], early_count[4]),
        out_shape=[result((half, width), BF16), result((LANES, half), F32), *shapes[4]],
        in_specs=[VMEM] * 4 + [HBM] * 2,
        out_specs=[VMEM] * (2 + len(shapes[4])),
        scratch_shapes=[
            pltpu.VMEM((kv_count, half, feats), F32),
            pltpu.VMEM((half, LANES), F32),
            early_sems[4],
        ],
        compiler_params=pltpu.CompilerParams(vmem_limit_bytes=16 * MIB),
        name="fetch",
    )(near(own), near(chosen), near(gain), near(router_rows), gate_rows, up_rows)
    early = early + more
    mine, theirs = pl.pallas_call(
        functools.partial(expert_kernel, per_unit, len(early)),
        out_shape=[result((kv_count * chips, rows, feats), BF16)] * 2,
        in_specs=[VMEM] * 6 + [HBM] * 3 + [VMEM] * len(early),
        out_specs=[VMEM] * 2,
        scratch_shapes=[
            pltpu.VMEM((3 * units - sum(early_count), unit_width, width), BF16),
            pltpu.VMEM((kv_count, half, feats), F32),
            pltpu.VMEM((half, LANES), F32),
            pltpu.VMEM((half, width), BF16),
            pltpu.VMEM((LANES, half), F32),
            pltpu.VMEM((LANES, all_rows), F32),
            pltpu.VMEM((units, unit_width, all_rows), BF16),
            pltpu.VMEM((kv_count, all_rows, feats), F32),
            pltpu.SemaphoreType.DMA((3 * units,)),
        ],
        compiler_params=pltpu.CompilerParams(vmem_limit_bytes=expert_room),
        cost_estimate=pl.CostEstimate(
            flops=6 * all_rows * halves * half_width * width,
            bytes_accessed=6 * halves * half_width * width,
            transcendentals=0,
        ),
        name="experts",
    )(
        near(other),
        near(norm_own),
        near(share_own),
        near(chosen),
        near(gain),
        near(router_rows),
        gate_rows,
        up_rows,
        down_rows,
        *[pinned(block) for block in early],
    )
    swapped = lax.ppermute(theirs, "core", ((0, 1), (1, 0)))
    both = pl.pallas_call(
        add_kernel,
        out_shape=result(mine.shape, BF16),
        in_specs=[VMEM] * 2,
        out_specs=VMEM,
        name="add",
    )(near(mine), near(swapped))
    returned = sent(both, ("kv", "z"))
    return pl.pallas_call(
        finish_kernel,
        out_shape=jax.ShapeDtypeStruct(stream_in.shape, BF16),
        in_specs=[VMEM] * 2,
        out_specs=VMEM,
        name="finish",
    )(near(returned), near(residual))


def solution(mesh):
    kv_count, wide_count = mesh.devices.shape
    split = Mesh(mesh.devices.reshape(kv_count, wide_count // 2, 2), ("kv",) + WIDE)
    return jax.shard_map(
        local,
        mesh=split,
        in_specs=(
            P(WIDE, None, "kv"),
            P(WIDE, None, "kv"),
            P(WIDE, None, None, "kv"),
            P("kv", WIDE, None, None),
            P("kv", WIDE, None, None),
            P(),
            P(),
            P(),
            P(WIDE, None, None),
            P(),
            P(),
            P(WIDE, None, "kv"),
            P(WIDE, None, "kv"),
            P(WIDE, "kv", None),
        ),
        out_specs=P(WIDE, None, "kv"),
        check_vma=False,
    )
```
